128 devices in a mesh: expert: 16 (over z, y), dp: 8 (over x, core).
Axes of the slice: x: 4, y: 4, z: 4, core: 2. Of those that a mesh axis runs over, the one named last changes fastest.
Arguments:
- tokens: bfloat16 [32768, 2048], P(('expert', 'dp')), may hold values from -6 to 6
- grad_out: bfloat16 [32768, 2048], P(('expert', 'dp')), may hold values from -3 to 3
- scores: float32 [32, 128], P('expert'), may hold values from 0.2 to 1
- chosen: int32 [32, 128], replicated, may hold values from 0 to 32767, as said below
- gate_vals: bfloat16 [32, 64, 2, 128, 128], P('expert', 'dp'), may hold values from -0.375 to 0.375
- up_vals: bfloat16 [32, 64, 2, 128, 128], P('expert', 'dp'), may hold values from -0.375 to 0.375
- down_vals: bfloat16 [32, 64, 2, 128, 128], P('expert', 'dp'), may hold values from -0.375 to 0.375
- gate_rows: int32 [32, 64, 2], P('expert', 'dp'), may hold values from 0 to 15, all different within a row
- down_cols: int32 [32, 64, 2], P('expert', 'dp'), may hold values from 0 to 15, all different within a row
Outputs:
- grad_tokens: bfloat16 [32768, 2048], P(('expert', 'dp'))
- grad_gate: float32 [32, 64, 2, 128, 128], P('expert', 'dp')
- grad_up: float32 [32, 64, 2, 128, 128], P('expert', 'dp')
- grad_down: float32 [32, 64, 2, 128, 128], P('expert', 'dp')
- grad_scores: float32 [32, 128], P('expert')
The draws below stay inside these ranges and needn't reach their ends.
Inputs may be any that keep to these rules, and one draw needn't show every extreme that they name: `chosen`: each row is ascending without repeats. Expert e takes between 0 and 2 tokens from the 256 tokens of one device (rows d * 256 to (d + 1) * 256 - 1), and exactly 2 from at least one device.
All inputs are finite; a program needn't handle non-finite values.
Results may differ from the reference program's by a relative error of at most 0.0057.
Values may be sent and summed in bfloat16 or wider, within the bound.
A program may use at most 128 MiB of HBM per device.

```python
import math
import jax
import jax.numpy as jnp
from jax import lax

D = 2048
BLK = 128
KB = 2
HB = 64
EXPERTS = 32
CAP = 128
TOK_DEV = 256
TOKENS = 32768
SLOT = 2
DEVICES = 128


def draw_chosen(key, part):
    key = jax.random.fold_in(key, 7)

    def one_expert(expert_key):
        sub_keys = jax.random.split(expert_key, 4)
        device_order = jax.random.permutation(sub_keys[0], DEVICES)
        pair_total = DEVICES // 2
        first_share = jax.random.randint(sub_keys[1], (pair_total,), 0, SLOT + 1)
        full_pair = jax.random.randint(sub_keys[2], (), 0, pair_total)
        first_share = jnp.where(jnp.arange(pair_total) == full_pair, SLOT, first_share)
        paired = jnp.stack([first_share, SLOT - first_share], axis=1).reshape(DEVICES).astype(jnp.int32)
        counts = jnp.zeros((DEVICES,), jnp.int32).at[device_order].set(paired)
        lane_ids = jnp.arange(SLOT)

        def pick_rows(device_key, count_here):
            picked = jax.random.permutation(device_key, TOK_DEV)[:SLOT]
            return jnp.sort(jnp.where(lane_ids < count_here, picked, TOK_DEV))
        picked_all = jax.vmap(pick_rows)(jax.random.split(sub_keys[3], DEVICES), counts)
        live_lane = lane_ids[None, :] < counts[:, None]
        starts = jnp.cumsum(counts) - counts
        target = jnp.where(live_lane, starts[:, None] + lane_ids[None, :], CAP)
        global_ids = (jnp.arange(DEVICES)[:, None] * TOK_DEV + picked_all).astype(jnp.int32)
        return jnp.zeros((CAP,), jnp.int32).at[target.reshape(-1)].set(global_ids.reshape(-1), mode='drop')
    return jax.vmap(one_expert)(jax.random.split(key, EXPERTS))


def levels(rng, dims, cuts, smallest, largest):
    factor_of, own = 1.0, jax.random.fold_in(rng, 6)
    for axis_at, shards_of in cuts:
        heights = jnp.exp(jax.random.uniform(jax.random.fold_in(own, axis_at), (shards_of,), jnp.float32, smallest / len(cuts), largest / len(cuts)))
        factor_of = factor_of * jnp.repeat(heights, dims[axis_at] // shards_of).reshape([-1 if axis == axis_at else 1 for axis in range(len(dims))])
    return factor_of


def picks_of(stream_key, rows, number_of, top, lift):
    order = jax.random.permutation(jax.random.fold_in(stream_key, 1), number_of)
    boost = order
    for power in range(3):
        boost = boost * boost // number_of
    boost = boost * lift // number_of
    chance = jax.random.randint(jax.random.fold_in(stream_key, 2), (rows, number_of), 0, 4096) + boost
    sure = jax.random.permutation(jax.random.fold_in(stream_key, 3), rows)[jnp.arange(number_of) % rows]
    chance = jnp.where(jnp.arange(rows)[:, None] == sure[None, :], 1 << 14, chance)
    priority = chance * number_of + jnp.arange(number_of)
    return lax.top_k(priority.astype(jnp.int32), top)[1].astype(jnp.int32)


def centred(stream_key, extent, spread, limit, cuts=(), kind=jnp.bfloat16):
    gain = levels(stream_key, extent, cuts, -0.22, 0.18) if cuts else 1.0
    result = jax.random.normal(stream_key, extent, jnp.float32) * spread * gain
    return jnp.minimum(jnp.maximum(result, -limit), limit).astype(kind)


def setup_inputs(seed: int = 0) -> dict:
    key_of = jax.random.split(jax.random.key(seed), 10)
    return {
        "tokens": centred(key_of[0], (TOKENS, D), 1.0, 6.0, ((0, 128),)),
        "grad_out": centred(key_of[1], (TOKENS, D), 0.5, 3.0, ((0, 128),)),
        "scores": jnp.clip(jnp.exp(math.log(1.0) - 1.609438 * jax.random.uniform(key_of[2], (EXPERTS, CAP), jnp.float32) ** levels(key_of[2], (EXPERTS, CAP), ((0, 16),), -0.2, 0.2)), 0.2, 1.0),
        "chosen": draw_chosen(jax.random.fold_in(key_of[9], 71), 0),
        "gate_vals": centred(key_of[4], (EXPERTS, HB, KB, BLK, BLK), (KB * BLK) ** -0.5, 0.375, ((0, 16), (1, 8))),
        "up_vals": centred(key_of[5], (EXPERTS, HB, KB, BLK, BLK), (KB * BLK) ** -0.5, 0.375, ((0, 16), (1, 8))),
        "down_vals": centred(key_of[6], (EXPERTS, HB, KB, BLK, BLK), (KB * BLK) ** -0.5, 0.375, ((0, 16), (1, 8))),
        "gate_rows": picks_of(key_of[7], EXPERTS * HB, D // BLK, KB, 0).reshape((EXPERTS, HB, KB)),
        "down_cols": picks_of(key_of[8], EXPERTS * HB, D // BLK, KB, 0).reshape((EXPERTS, HB, KB)),
    }


def rounded(value):
    return lax.optimization_barrier(value.astype(jnp.bfloat16)).astype(jnp.float32)


def expert_pass(rows_in, rows_grad, row_scores, gate_block, up_block, down_block, in_blocks, out_blocks):
    row_count, feat_width = rows_in.shape
    hid_blocks, link_count, block_size, _ = gate_block.shape
    block_count = feat_width // block_size
    high = lax.Precision.HIGHEST
    picked_in = jnp.take(rows_in.reshape(row_count, block_count, block_size), in_blocks.reshape(-1), axis=1)
    picked_in = picked_in.reshape(row_count, hid_blocks, link_count, block_size).astype(jnp.float32)
    picked_out = jnp.take(rows_grad.reshape(row_count, block_count, block_size), out_blocks.reshape(-1), axis=1)
    picked_out = picked_out.reshape(row_count, hid_blocks, link_count, block_size).astype(jnp.float32)
    gate_w = gate_block.astype(jnp.float32)
    up_w = up_block.astype(jnp.float32)
    down_w = down_block.astype(jnp.float32)
    gate_pre = jnp.einsum('rhkc,hkcf->rhf', picked_in, gate_w, precision=high)
    up_pre = jnp.einsum('rhkc,hkcf->rhf', picked_in, up_w, precision=high)
    gate_sig = jax.nn.sigmoid(gate_pre)
    gate_act = gate_pre * gate_sig
    hidden = rounded(gate_act * up_pre)
    out_terms = jnp.einsum('rhf,hkfc->rhkc', hidden, down_w, precision=high)
    score_grad = jnp.sum(picked_out * out_terms, axis=(1, 2, 3))
    scaled = rounded(row_scores[:, None, None, None] * picked_out)
    hidden_back = jnp.einsum('rhkc,hkfc->rhf', scaled, down_w, precision=high)
    down_grad = jnp.einsum('rhf,rhkc->hkfc', hidden, scaled, precision=high)
    up_back = rounded(hidden_back * gate_act)
    gate_back = rounded(hidden_back * up_pre * gate_sig * (1.0 + gate_pre * (1.0 - gate_sig)))
    gate_grad = jnp.einsum('rhkc,rhf->hkcf', picked_in, gate_back, precision=high)
    up_grad = jnp.einsum('rhkc,rhf->hkcf', picked_in, up_back, precision=high)
    in_terms = jnp.einsum('rhf,hkcf->rhkc', gate_back, gate_w, precision=high)
    in_terms = in_terms + jnp.einsum('rhf,hkcf->rhkc', up_back, up_w, precision=high)
    input_grad = jnp.zeros((row_count, block_count, block_size), in_terms.dtype)
    input_grad = input_grad.at[:, in_blocks.reshape(-1)].add(in_terms.reshape(row_count, hid_blocks * link_count, block_size))
    return input_grad.reshape(row_count, feat_width), gate_grad, up_grad, down_grad, score_grad


def reference(tokens, grad_out, scores, chosen, gate_vals, up_vals, down_vals, gate_rows, down_cols):
    def one_step(total, item):
        picked, weights, gate_block, up_block, down_block, in_blocks, out_blocks = item
        input_grad, gate_grad, up_grad, down_grad, score_grad = expert_pass(
            tokens[picked], grad_out[picked], weights, gate_block, up_block, down_block, in_blocks, out_blocks)
        return total.at[picked].add(input_grad), (gate_grad, up_grad, down_grad, score_grad)

    initial = jnp.zeros(tokens.shape, jnp.float32)
    total, (grad_gate, grad_up, grad_down, grad_scores) = lax.scan(
        one_step, initial, (chosen, scores, gate_vals, up_vals, down_vals, gate_rows, down_cols))
    return total.astype(jnp.bfloat16), grad_gate, grad_up, grad_down, grad_scores
```

```python
import functools

import jax
import jax.numpy as jnp
from jax import lax
from jax.experimental import pallas as pl
from jax.experimental.pallas import tpu as pltpu
from jax.sharding import PartitionSpec as P

MESH = pl.DeviceIdType.MESH
BF, F32, I32 = jnp.bfloat16, jnp.float32, jnp.int32
RING = 4


def iota(shape, dim):
    return lax.broadcasted_iota(I32, shape, dim)


def as_bf(mask):
    return jnp.where(mask, 1.0, 0.0).astype(BF)


def dot(a, b, dims=((1,), (0,))):
    return lax.dot_general(a, b, (dims, ((), ())), preferred_element_type=F32)


def same_int(a, b):
    return -(((a - b) * (a - b) - 1) >> 31)


def log2(n):
    return n.bit_length() - 1


def exchange(
    dims, chosen_ref, scores_ref, grows_ref, dcols_ref, tokens_hbm, grads_hbm, gate_hbm, up_hbm, down_hbm,
    xg_out, h_out, a_out, u_out, back_out, scol_out, hot_out, gs_out,
    tok_v, grd_v, gate_v, up_v, down_v, base_v, slot_v, gsum_v, terms_v, h_v, a_v, u_v, gsx_send, gsx_recv,
    send1_0, send1_1, recv1_0, recv1_1, gath_0, gath_1, part_0, part_1, sib_0, sib_1,
    hop_send, hop_recv, fst_v, send2, back_0, back_1,
    load_sem, out_sem, p1_send, p1_recv, ag_send, ag_recv, sib_send, sib_recv, rs_send, rs_recv,
    p2_send, p2_recv, gs_send, gs_recv,
):
    G, M, D, T, HB = dims
    E2 = 2 * G
    SR = 2 * G
    Q, O = D // 4, D // 8
    NB = D // 128
    send1, recv1 = (send1_0, send1_1), (recv1_0, recv1_1)
    gath, part, sib, back = (gath_0, gath_1), (part_0, part_1), (sib_0, sib_1), (back_0, back_1)

    e, d = lax.axis_index("expert"), lax.axis_index("dp")
    x, c = d // 2, d % 2
    oc = 1 - c
    right = (e, ((x + 1) % RING) * 2 + c)
    left = (e, ((x + 3) % RING) * 2 + c)
    sibling = (e, x * 2 + oc)
    b_own = c * RING + x
    b_right = c * RING + (x + 1) % RING
    b_left = c * RING + (x + 3) % RING
    b_opp = c * RING + (x + 2) % RING

    loads = []
    for k, (src, dst) in enumerate(
        ((tokens_hbm, tok_v), (grads_hbm, grd_v), (gate_hbm, gate_v), (up_hbm, up_v), (down_hbm, down_v))
    ):
        cp = pltpu.make_async_copy(src, dst, load_sem.at[k])
        cp.start()
        loads.append(cp)

    barrier = pltpu.get_barrier_semaphore()

    @pl.loop(1, G)
    def _(i):
        pl.semaphore_signal(barrier, inc=1, device_id=((e + i) % G, d), device_id_type=MESH)

    @pl.loop(1, M)
    def _(i):
        pl.semaphore_signal(barrier, inc=1, device_id=(e, (d + i) % M), device_id_type=MESH)

    chosen = chosen_ref[...]
    cap = chosen.shape[1]
    lo = (e * M + d) * T
    pos = iota(chosen.shape, 1)
    before = jnp.sum(jnp.where(chosen < lo, 1, 0), axis=1, keepdims=True)
    count = jnp.sum(jnp.where(chosen < lo + T, 1, 0), axis=1, keepdims=True) - before
    tok_id = iota((E2, T), 1)
    for j in range(2):
        loc = jnp.sum(jnp.where(pos == before + j, chosen, 0), axis=1, keepdims=True) - lo
        loc = jnp.where(count > j, loc, -1)
        hot_out[j * E2 : (j + 1) * E2, :] = as_bf(tok_id == loc)
    owner = lax.shift_right_logical(chosen, log2(T))
    same = jnp.where((pltpu.roll(owner, 1, 1) == owner) & (pos > 0), 1, 0)
    member = owner & (M - 1)
    group = lax.shift_right_logical(owner, log2(M))
    slot_v[...] = ((member & 1) * RING + lax.shift_right_logical(member, 1)) * SR + group * 2 + same

    loads[0].wait()
    loads[1].wait()
    hot = hot_out[...]
    for arr, src in enumerate((tok_v, grd_v)):
        for q in range(4):
            base_v[arr * 4 + q] = dot(hot, src[:, q * Q : (q + 1) * Q]).astype(BF)

    def p1_copy(m, i):
        g = (e + i) % G
        return pltpu.make_async_remote_copy(
            src_ref=send1[m].at[g], dst_ref=recv1[m].at[e], send_sem=p1_send.at[m, i], recv_sem=p1_recv.at[m, i],
            device_id=(g, d), device_id_type=MESH,
        )

    def p2_copy(m, i):
        g = (e + i) % G
        return pltpu.make_async_remote_copy(
            src_ref=send2.at[m, g], dst_ref=back[m].at[e], send_sem=p2_send.at[m, i], recv_sem=p2_recv.at[m, i],
            device_id=(g, d), device_id_type=MESH,
        )

    stacked = base_v[...].reshape(8 * 2 * E2, Q)
    shape = (G * 16, 8 * 2 * E2)
    row, col = iota(shape, 0), iota(shape, 1)
    want = ((row >> 1) & 7) * (2 * E2) + (row & 1) * E2 + (row >> 4) * 2
    for m in range(2):
        send1[m][...] = dot(as_bf(col == want + m), stacked).astype(BF).reshape(G, 16, Q)
        if m == 0:
            pl.semaphore_wait(barrier, G - 1 + M - 1)
        recv1[m][e] = send1[m][e]

        @pl.loop(1, G)
        def _(i, m=m):
            p1_copy(m, i).start()

    def retile(m):
        @pl.loop(1, G)
        def _(i):
            p1_copy(m, i).wait_recv()

        shape = (16 * G, 16 * G)
        row, col = iota(shape, 0), iota(shape, 1)
        q = row >> log2(4 * G)
        arr = (row >> log2(2 * G)) & 1
        src = (row >> 1) & (G - 1)
        pick = as_bf(col == src * 16 + arr * 8 + q * 2 + (row & 1))
        out = dot(pick, recv1[m][...].reshape(16 * G, Q)).astype(BF)
        per_q = NB // 4
        for q in range(4):
            for i in range(per_q):
                gath[m][q * per_q + i, b_own] = out[q * 4 * G : (q + 1) * 4 * G, i * 128 : (i + 1) * 128]

    XR, GR = pl.ds(0, SR), pl.ds(SR, SR)

    def ag(m, k):
        b, rows, to = (
            (b_own, XR, right), (b_own, GR, right), (b_own, GR, left), (b_own, XR, left),
            (b_left, XR, right), (b_right, GR, left),
        )[k]
        ref = gath[m].at[:, b, rows]
        return pltpu.make_async_remote_copy(
            src_ref=ref, dst_ref=ref, send_sem=ag_send.at[m, k], recv_sem=ag_recv.at[m, k],
            device_id=to, device_id_type=MESH,
        )

    def sb(m, k):
        b, rows = (
            (b_own, XR), (b_own, GR), (b_left, XR), (b_left, GR), (b_right, GR), (b_right, XR), (b_opp, XR), (b_opp, GR),
        )[k]
        ref = gath[m].at[:, b, rows]
        return pltpu.make_async_remote_copy(
            src_ref=ref, dst_ref=ref, send_sem=sib_send.at[m, k], recv_sem=sib_recv.at[m, k],
            device_id=sibling, device_id_type=MESH,
        )

    def ag_start(m):
        for k in (0, 2, 1, 3):
            ag(m, k).start()
        sb(m, 0).start()
        sb(m, 1).start()

    def ag_relay(m):
        ag(m, 0).wait_recv()
        ag(m, 4).start()
        sb(m, 2).start()
        ag(m, 2).wait_recv()
        ag(m, 5).start()
        sb(m, 4).start()
        ag(m, 1).wait_recv()
        sb(m, 3).start()
        ag(m, 3).wait_recv()
        sb(m, 5).start()

    def ag_finish(m):
        ag(m, 4).wait_recv()
        sb(m, 6).start()
        ag(m, 5).wait_recv()
        sb(m, 7).start()
        for k in range(8):
            sb(m, k).wait_recv()
        pltpu.make_async_copy(gath[m], xg_out.at[m], out_sem.at[m, 0]).start()

    def weights(m, h):
        both = [
            jnp.concatenate([w[m, h, 0], w[m, h, 1]], axis=0) for w in (gate_v, up_v)
        ]
        return jnp.concatenate(both, axis=1)

    def picked(m, h, refs, lo_row):
        out = []
        for k in range(2):
            block = gath[m][refs[m, h, k], :, lo_row : lo_row + SR]
            out.append(block.reshape(M * SR, 128))
        return out

    def compute(m):
        mask = iota((M * SR, cap), 0) == slot_v[pl.ds(2 * e + m, 1), :]
        s = jnp.sum(jnp.where(mask, scores_ref[pl.ds(m, 1), :], 0.0), axis=1, keepdims=True)
        scol_out[m] = jnp.broadcast_to(s, (M * SR, 128))
        gsum_v[...] = jnp.zeros_like(gsum_v)

        @pl.loop(0, HB)
        def _(h):
            w = weights(m, h)
            ab = dot(jnp.concatenate(picked(m, h, grows_ref, 0), axis=1), w)
            a, b = ab[:, :128], ab[:, 128:]
            gk = picked(m, h, dcols_ref, SR)
            t = dot(gk[0], down_v[m, h, 0], ((1,), (1,))) + dot(gk[1], down_v[m, h, 1], ((1,), (1,)))
            sig = jax.nn.sigmoid(a)
            act = a * sig
            hid = (act * b).astype(BF)
            gsum_v[...] += hid.astype(F32) * t
            q = t * scol_out[m]
            ub = (q * act).astype(BF)
            ga = (q * b * sig * (1.0 + a * (1.0 - sig))).astype(BF)
            h_v[m, h] = hid
            a_v[m, h] = ga
            u_v[m, h] = ub
            r = dot(jnp.concatenate([ga, ub], axis=1), w, ((1,), (1,)))
            terms_v[2 * h] = r[:, :128]
            terms_v[2 * h + 1] = r[:, 128:]

        for k, (src, dst) in enumerate(((h_v, h_out), (a_v, a_out), (u_v, u_out))):
            pltpu.make_async_copy(src.at[m], dst.at[m], out_sem.at[m, k + 1]).start()
        total = jnp.sum(gsum_v[...], axis=1, keepdims=True)
        gsx_send[m : m + 1, :cap] = jnp.sum(jnp.where(mask, total, 0.0), axis=0, keepdims=True)

        @pl.loop(0, NB)
        def _(f):
            acc = jnp.zeros((M * SR, 128), F32)
            for h in range(HB):
                n0 = same_int(grows_ref[m, h, 0], f)
                n1 = (1 - n0) * same_int(grows_ref[m, h, 1], f)
                acc += terms_v[2 * HB - n0 * (2 * HB - 2 * h) - n1 * (2 * HB - 2 * h - 1)]
            part[m][:, :, pl.ds(pl.multiple_of(f * 128, 128), 128)] = acc.astype(BF).reshape(M, SR, 128)

        core_copy(m).start()

    def core_copy(m):
        return pltpu.make_async_remote_copy(
            src_ref=part[m].at[pl.ds(oc * RING, RING)], dst_ref=sib[m], send_sem=sib_send.at[m, 8],
            recv_sem=sib_recv.at[m, 8], device_id=sibling, device_id_type=MESH,
        )

    HA, HBH = slice(0, D // 2), slice(D // 2, D)

    def rs_copy(m, k):
        return pltpu.make_async_remote_copy(
            src_ref=hop_send.at[m, k], dst_ref=hop_recv.at[m, k], send_sem=rs_send.at[m, k],
            recv_sem=rs_recv.at[m, k], device_id=left if k % 2 else right, device_id_type=MESH,
        )

    def pair_sum(m, step, lanes):
        xx = (x + step) % RING
        return part[m][c * RING + xx, :, lanes].astype(F32) + sib[m][xx, :, lanes].astype(F32)

    def rs_start(m):
        core_copy(m).wait_recv()
        for k, step, lanes in ((0, 2, HA), (1, 2, HBH), (2, 1, HBH), (3, 3, HA)):
            hop_send[m, k] = pair_sum(m, step, lanes).astype(BF)
            rs_copy(m, k).start()

    def rs_middle(m):
        for k, step, lanes in ((4, 1, HA), (5, 3, HBH)):
            rs_copy(m, k - 4).wait_recv()
            hop_send[m, k] = (pair_sum(m, step, lanes) + hop_recv[m, k - 4].astype(F32)).astype(BF)
            rs_copy(m, k).start()

    def rs_finish(m):
        for k in (2, 3, 4, 5):
            rs_copy(m, k).wait_recv()
        fin_a = pair_sum(m, 0, HA) + hop_recv[m, 4].astype(F32) + hop_recv[m, 3].astype(F32)
        fin_b = pair_sum(m, 0, HBH) + hop_recv[m, 2].astype(F32) + hop_recv[m, 5].astype(F32)
        for o in range(4):
            fst_v[o] = fin_a[:, o * O : (o + 1) * O].astype(BF)
            fst_v[o + 4] = fin_b[:, o * O : (o + 1) * O].astype(BF)
        shape = (16 * G, 8 * SR)
        row, col = iota(shape, 0), iota(shape, 1)
        pick = as_bf(col == ((row >> 1) & 7) * SR + (row >> 4) * 2 + (row & 1))
        send2[m] = dot(pick, fst_v[...].reshape(8 * SR, O)).astype(BF).reshape(G, 16, O)
        back[m][e] = send2[m, e]

        @pl.loop(1, G)
        def _(i):
            p2_copy(m, i).start()

    def return_finish(m):
        @pl.loop(1, G)
        def _(i):
            p2_copy(m, i).wait_recv()

        pltpu.make_async_copy(back[m], back_out.at[m], out_sem.at[m, 4]).start()

    def gs_copy(i):
        return pltpu.make_async_remote_copy(
            src_ref=gsx_send, dst_ref=gsx_recv.at[d], send_sem=gs_send.at[i], recv_sem=gs_recv.at[i],
            device_id=(e, (d + i) % M), device_id_type=MESH,
        )

    terms_v[2 * HB] = jnp.zeros((M * SR, 128), F32)
    gsx_send[...] = jnp.zeros_like(gsx_send)
    retile(0)
    ag_start(0)
    retile(1)
    ag_relay(0)
    ag_start(1)
    ag_finish(0)
    for cp in loads[2:]:
        cp.wait()
    compute(0)
    ag_relay(1)
    rs_start(0)
    ag_finish(1)
    rs_middle(0)
    compute(1)
    gsx_recv[d] = gsx_send[...]

    @pl.loop(1, M)
    def _(i):
        gs_copy(i).start()

    rs_finish(0)
    rs_start(1)
    rs_middle(1)
    return_finish(0)
    rs_finish(1)

    @pl.loop(1, M)
    def _(i):
        gs_copy(i).wait_recv()

    gs = gsx_recv[0]
    for i in range(1, M):
        gs = gs + gsx_recv[i]
    gs_out[...] = gs[:2, :cap]
    return_finish(1)

    for m in range(2):

        @pl.loop(1, G)
        def _(i, m=m):
            p1_copy(m, i).wait_send()
            p2_copy(m, i).wait_send()

        for k in range(6):
            ag(m, k).wait_send()
            rs_copy(m, k).wait_send()
        for k in range(8):
            sb(m, k).wait_send()
        core_copy(m).wait_send()
        for k, (src, dst) in enumerate(
            ((gath[m], xg_out), (h_v.at[m], h_out), (a_v.at[m], a_out), (u_v.at[m], u_out), (back[m], back_out))
        ):
            pltpu.make_async_copy(src, dst.at[m], out_sem.at[m, k]).wait()

    @pl.loop(1, M)
    def _(i):
        gs_copy(i).wait_send()


def block_grads(
    dims, per_step, grows_ref, dcols_ref, xg_ref, h_ref, a_ref, u_ref, back_ref, scol_ref, hot_ref,
    gt_ref, gg_ref, gu_ref, gd_ref,
):
    G, M, D, T, HB = dims
    E2, SR, O = 2 * G, 2 * G, D // 8
    m, step = pl.program_id(0), pl.program_id(1)

    def picked(h, refs, lo_row):
        out = []
        for k in range(2):
            out.append(xg_ref[0, refs[m, h, k], :, lo_row : lo_row + SR].reshape(M * SR, 128))
        return out

    for i in range(per_step):
        h = step * per_step + i
        xx = jnp.concatenate(picked(h, grows_ref, 0), axis=1)
        au = jnp.concatenate([a_ref[0, i], u_ref[0, i]], axis=1)
        both = dot(xx, au, ((0,), (0,)))
        scol = scol_ref[0]
        pp = jnp.concatenate([(g.astype(F32) * scol).astype(BF) for g in picked(h, dcols_ref, SR)], axis=1)
        down = dot(h_ref[0, i], pp, ((0,), (0,)))
        for k in range(2):
            gg_ref[0, i, k] = both[k * 128 : (k + 1) * 128, :128]
            gu_ref[0, i, k] = both[k * 128 : (k + 1) * 128, 128:]
            gd_ref[0, i, k] = down[:, k * 128 : (k + 1) * 128]

    @pl.when((m == 0) & (step == 0))
    def _():
        shape = (8 * 2 * E2, 2 * 16 * G)
        row, col = iota(shape, 0), iota(shape, 1)
        o, j = row >> log2(2 * E2), (row >> log2(E2)) & 1
        g, mm = (row >> 1) & (G - 1), row & 1
        pick = as_bf(col == mm * (16 * G) + g * 16 + o * 2 + j)
        vals = dot(pick, back_ref[...].reshape(2 * 16 * G, O)).astype(BF)
        for o in range(8):
            block = vals[o * 2 * E2 : (o + 1) * 2 * E2]
            gt_ref[:, o * O : (o + 1) * O] = dot(hot_ref[...], block, ((0,), (0,))).astype(BF)


def on_device(tokens, grad_out, scores, chosen, gate_vals, up_vals, down_vals, gate_rows, down_cols):
    G, M = lax.axis_size("expert"), lax.axis_size("dp")
    T, D = tokens.shape
    HB = gate_vals.shape[1]
    cap = chosen.shape[1]
    dims = (G, M, D, T, HB)
    SR, O, Q = 2 * G, D // 8, D // 4
    rows = M * SR
    hbm, vmem, smem = (pl.BlockSpec(memory_space=s) for s in (pl.ANY, pltpu.VMEM, pltpu.SMEM))
    dma = pltpu.SemaphoreType.DMA
    sds = jax.ShapeDtypeStruct
    xg, hid, ga, ub, back, scol, hot, gs = pl.pallas_call(
        functools.partial(exchange, dims),
        out_shape=(
            sds((2, D // 128, M, 2 * SR, 128), BF),
            sds((2, HB, rows, 128), BF),
            sds((2, HB, rows, 128), BF),
            sds((2, HB, rows, 128), BF),
            sds((2, G, 16, O), BF),
            sds((2, rows, 128), F32),
            sds((4 * G, T), BF),
            sds((2, cap), F32),
        ),
        in_specs=[vmem, vmem, smem, smem] + [hbm] * 5,
        out_specs=(hbm,) * 5 + (vmem,) * 3,
        scratch_shapes=[
            pltpu.VMEM((T, D), BF),
            pltpu.VMEM((T, D), BF),
            pltpu.VMEM(gate_vals.shape, BF),
            pltpu.VMEM(gate_vals.shape, BF),
            pltpu.VMEM(gate_vals.shape, BF),
            pltpu.VMEM((8, 4 * G, Q), BF),
            pltpu.VMEM(chosen.shape, I32),
            pltpu.VMEM((rows, 128), F32),
            pltpu.VMEM((2 * HB + 1, rows, 128), F32),
            pltpu.VMEM((2, HB, rows, 128), BF),
            pltpu.VMEM((2, HB, rows, 128), BF),
            pltpu.VMEM((2, HB, rows, 128), BF),
            pltpu.VMEM((8, 128), F32),
            pltpu.VMEM((M, 8, 128), F32),
            pltpu.VMEM((G, 16, Q), BF),
            pltpu.VMEM((G, 16, Q), BF),
            pltpu.VMEM((G, 16, Q), BF),
            pltpu.VMEM((G, 16, Q), BF),
            pltpu.VMEM((D // 128, M, 2 * SR, 128), BF),
            pltpu.VMEM((D // 128, M, 2 * SR, 128), BF),
            pltpu.VMEM((M, SR, D), BF),
            pltpu.VMEM((M, SR, D), BF),
            pltpu.VMEM((RING, SR, D), BF),
            pltpu.VMEM((RING, SR, D), BF),
            pltpu.VMEM((2, 6, SR, D // 2), BF),
            pltpu.VMEM((2, 6, SR, D // 2), BF),
            pltpu.VMEM((8, SR, O), BF),
            pltpu.VMEM((2, G, 16, O), BF),
            pltpu.VMEM((G, 16, O), BF),
            pltpu.VMEM((G, 16, O), BF),
            dma((5,)),
            dma((2, 5)),
            dma((2, G)),
            dma((2, G)),
            dma((2, 6)),
            dma((2, 6)),
            dma((2, 9)),
            dma((2, 9)),
            dma((2, 6)),
            dma((2, 6)),
            dma((2, G)),
            dma((2, G)),
            dma((M,)),
            dma((M,)),
        ],
        compiler_params=pltpu.CompilerParams(
            collective_id=0, has_side_effects=True, vmem_limit_bytes=44 * 1024 * 1024
        ),
        name="exchange",
    )(chosen, scores, gate_rows, down_cols, tokens, grad_out, gate_vals, up_vals, down_vals)

    per_step = 2
    spec = pl.BlockSpec

    def by_step(*tail):
        return spec((1, per_step) + tail, lambda m, i, *_: (m, i) + (0,) * len(tail))

    def by_member(*tail):
        return spec((1,) + tail, lambda m, i, *_: (m,) + (0,) * len(tail))

    def whole(*shape):
        return spec(shape, lambda m, i, *_: (0,) * len(shape))

    grads = sds(gate_vals.shape, F32)
    grad_tokens, grad_gate, grad_up, grad_down = pl.pallas_call(
        functools.partial(block_grads, dims, per_step),
        out_shape=(sds((T, D), BF), grads, grads, grads),
        grid_spec=pltpu.PrefetchScalarGridSpec(
            num_scalar_prefetch=2,
            grid=(2, HB // per_step),
            in_specs=[
                by_member(D // 128, M, 2 * SR, 128),
                by_step(rows, 128),
                by_step(rows, 128),
                by_step(rows, 128),
                whole(2, G, 16, O),
                by_member(rows, 128),
                whole(4 * G, T),
            ],
            out_specs=(
                whole(T, D),
                by_step(2, 128, 128),
                by_step(2, 128, 128),
                by_step(2, 128, 128),
            ),
        ),
        compiler_params=pltpu.CompilerParams(vmem_limit_bytes=40 * 1024 * 1024),
        name="block_grads",
    )(gate_rows, down_cols, xg, hid, ga, ub, back, scol, hot)
    return grad_tokens, grad_gate, grad_up, grad_down, gs


def solution(mesh):
    rows = P(("expert", "dp"), None)
    blocks = P("expert", "dp", None, None, None)
    links = P("expert", "dp", None)
    return jax.shard_map(
        on_device,
        mesh=mesh,
        in_specs=(rows, rows, P("expert", None), P(), blocks, blocks, blocks, links, links),
        out_specs=(rows, blocks, blocks, blocks, P("expert", None)),
        check_vma=False,
    )
```

```python
import functools

import jax
import jax.numpy as jnp
from jax import lax
from jax.experimental import pallas as pl
from jax.experimental.pallas import tpu as pltpu
from jax.sharding import PartitionSpec as P

MESH = pl.DeviceIdType.MESH
BF, F32, I32 = jnp.bfloat16, jnp.float32, jnp.int32
RING = 4


def iota(shape, dim):
    return lax.broadcasted_iota(I32, shape, dim)


def as_bf(mask):
    return jnp.where(mask, 1.0, 0.0).astype(BF)


def dot(a, b, dims=((1,), (0,))):
    return lax.dot_general(a, b, (dims, ((), ())), preferred_element_type=F32)


def same_int(a, b):
    return -(((a - b) * (a - b) - 1) >> 31)


def log2(n):
    return n.bit_length() - 1


def exchange(
    dims, chosen_hbm, scores_hbm, grows_hbm, dcols_hbm, tokens_hbm, grads_hbm, gate_hbm, up_hbm, down_hbm,
    gt_out, gg_out, gu_out, gd_out, gs_out,
    chosen_v, scores_v, grows_s, dcols_s, table_s, tok_v, grd_v, gate_v, up_v, down_v, wt_v, dt_v, hot_v, hotm_v, base_v,
    slot_v, scol_v, gsum_v, terms_v, h_v, a_v, u_v, p_v, gsx_send, gsx_recv, gt_v,
    send1_0, send1_1, recv1_0, recv1_1, gath_0, gath_1, part_0, part_1, own_0, own_1, sib_0, sib_1,
    hop_send, hop_recv, fst_v, send2, back_0, back_1,
    load_sem, p1_send, p1_recv, ag_send, ag_recv, sib_send, sib_recv, rs_send, rs_recv,
    p2_send, p2_recv, gs_send, gs_recv,
):
    G, M, D, T, HB = dims
    E2 = 2 * G
    SR = 2 * G
    Q, O = D // 4, D // 8
    NB = D // 128
    send1, recv1 = (send1_0, send1_1), (recv1_0, recv1_1)
    gath, part, own = (gath_0, gath_1), (part_0, part_1), (own_0, own_1)
    sib, back = (sib_0, sib_1), (back_0, back_1)

    e, d = lax.axis_index("expert"), lax.axis_index("dp")
    x, c = d // 2, d % 2
    oc = 1 - c
    right = (e, ((x + 1) % RING) * 2 + c)
    left = (e, ((x + 3) % RING) * 2 + c)
    sibling = (e, x * 2 + oc)
    b_own = c * RING + x
    b_right = c * RING + (x + 1) % RING
    b_left = c * RING + (x + 3) % RING
    b_opp = c * RING + (x + 2) % RING

    barrier = pltpu.get_barrier_semaphore()

    @pl.loop(1, G)
    def _(i):
        pl.semaphore_signal(barrier, inc=1, device_id=((e + i) % G, d), device_id_type=MESH)

    @pl.loop(1, M)
    def _(i):
        pl.semaphore_signal(barrier, inc=1, device_id=(e, (d + i) % M), device_id_type=MESH)

    loads = []
    for k, (src, dst) in enumerate((
        (chosen_hbm, chosen_v), (tokens_hbm, tok_v), (grads_hbm, grd_v), (scores_hbm, scores_v), (grows_hbm, grows_s),
        (dcols_hbm, dcols_s), (gate_hbm, gate_v), (up_hbm, up_v), (down_hbm, down_v),
    )):
        loads.append(pltpu.make_async_copy(src, dst, load_sem.at[k]))
    for cp in loads[:6]:
        cp.start()

    loads[0].wait()
    chosen = chosen_v[...]
    cap = chosen.shape[1]
    lo = (e * M + d) * T
    pos = iota(chosen.shape, 1)
    before = jnp.sum(jnp.where(chosen < lo, 1, 0), axis=1, keepdims=True)
    count = jnp.sum(jnp.where(chosen < lo + T, 1, 0), axis=1, keepdims=True) - before
    tok_id = iota((E2, T), 1)
    for j in range(2):
        loc = jnp.sum(jnp.where(pos == before + j, chosen, 0), axis=1, keepdims=True) - lo
        loc = jnp.where(count > j, loc, -1)
        hot_v[j * E2 : (j + 1) * E2, :] = as_bf(tok_id == loc)

    hot = hot_v[...]
    for arr, src in enumerate((tok_v, grd_v)):
        loads[1 + arr].wait()
        for q in range(4):
            base_v[arr * 4 + q] = dot(hot, src[:, q * Q : (q + 1) * Q]).astype(BF)

    arriving, leaving = {}, []

    def go(make, *key):
        make(*key).start()
        arriving[make, key] = lambda: make(*key).wait_recv()
        leaving.append(lambda: make(*key).wait_send())

    def go_all(make, n, *key):
        @pl.loop(1, n)
        def _(i):
            make(*key, i).start()

        def arrive():
            @pl.loop(1, n)
            def _(i):
                make(*key, i).wait_recv()

        def leave():
            @pl.loop(1, n)
            def _(i):
                make(*key, i).wait_send()

        arriving[make, key] = arrive
        leaving.append(leave)

    def got(make, *key):
        arriving.pop((make, key))()

    def p1_copy(m, i):
        g = (e + i) % G
        return pltpu.make_async_remote_copy(
            src_ref=send1[m].at[g], dst_ref=recv1[m].at[e], send_sem=p1_send.at[m, i], recv_sem=p1_recv.at[m, i],
            device_id=(g, d), device_id_type=MESH,
        )

    def p2_copy(m, i):
        g = (e + i) % G
        return pltpu.make_async_remote_copy(
            src_ref=send2.at[m, g], dst_ref=back[m].at[e], send_sem=p2_send.at[m, i], recv_sem=p2_recv.at[m, i],
            device_id=(g, d), device_id_type=MESH,
        )

    stacked = base_v[...].reshape(8 * 2 * E2, Q)
    shape = (G * 16, 8 * 2 * E2)
    row, col = iota(shape, 0), iota(shape, 1)
    want = ((row >> 1) & 7) * (2 * E2) + (row & 1) * E2 + (row >> 4) * 2
    for m in range(2):
        send1[m][...] = dot(as_bf(col == want + m), stacked).astype(BF).reshape(G, 16, Q)
        if m == 0:
            pl.semaphore_wait(barrier, G - 1 + M - 1)
        go_all(p1_copy, G, m)
        recv1[m][e] = send1[m][e]
    for cp in loads[6:]:
        cp.start()

    def prepare():
        owner = lax.shift_right_logical(chosen, log2(T))
        same = jnp.where((pltpu.roll(owner, 1, 1) == owner) & (pos > 0), 1, 0)
        member = owner & (M - 1)
        group = lax.shift_right_logical(owner, log2(M))
        slot_v[...] = ((member & 1) * RING + lax.shift_right_logical(member, 1)) * SR + group * 2 + same
        for cp in loads[3:6]:
            cp.wait()
        for m in range(2):
            s = jnp.sum(jnp.where(slot_mask(m), scores_v[m : m + 1, :], 0.0), axis=1, keepdims=True)
            scol_v[m] = jnp.broadcast_to(s, (M * SR, 128)).reshape(M, SR, 128)
            row, col = iota((E2, 2 * E2), 0), iota((E2, 2 * E2), 1)
            pick = as_bf(col == (row >> log2(G)) * E2 + (row & (G - 1)) * 2 + m)
            hotm_v[m] = dot(pick, hot_v[...]).astype(BF)

        @pl.loop(0, 2 * HB)
        def _(i):
            m, h = i // HB, i % HB
            g0, g1 = grows_s[m, 0, h], grows_s[m, 1, h]
            for f in range(NB):
                n0 = same_int(g0, f)
                n1 = (1 - n0) * same_int(g1, f)
                table_s[i * NB + f] = 2 * HB - n0 * (2 * HB - 2 * h) - n1 * (2 * HB - 2 * h - 1)

        for cp in loads[6:]:
            cp.wait()

        @pl.loop(0, 2 * HB)
        def _(i):
            m, h = i // HB, i % HB
            for k in range(2):
                span = slice(k * 128, (k + 1) * 128)
                wt_v[m, h, :128, span] = gate_v[m, h, k].T
                wt_v[m, h, 128:, span] = up_v[m, h, k].T
                dt_v[m, h, span, :] = down_v[m, h, k].T

        terms_v[2 * HB] = jnp.zeros((2, M // 2 * SR, 128), F32)
        gsx_send[...] = jnp.zeros_like(gsx_send)

    def slot_mask(m):
        return iota((M * SR, cap), 0) == slot_v[pl.ds(2 * e + m, 1), :]

    def retile(m):
        got(p1_copy, m)
        shape = (16 * G, 16 * G)
        row, col = iota(shape, 0), iota(shape, 1)
        q = row >> log2(4 * G)
        arr = (row >> log2(2 * G)) & 1
        src = (row >> 1) & (G - 1)
        pick = as_bf(col == src * 16 + arr * 8 + q * 2 + (row & 1))
        out = dot(pick, recv1[m][...].reshape(16 * G, Q)).astype(BF)
        per_q = NB // 4
        for q in range(4):
            for i in range(per_q):
                gath[m][q * per_q + i, b_own] = out[q * 4 * G : (q + 1) * 4 * G, i * 128 : (i + 1) * 128]

    XR, GR = pl.ds(0, SR), pl.ds(SR, SR)

    def ag(m, k):
        b, rows, to = (
            (b_own, XR, right), (b_own, GR, right), (b_own, GR, left), (b_own, XR, left),
            (b_left, XR, right), (b_right, GR, left),
        )[k]
        ref = gath[m].at[:, b, rows]
        return pltpu.make_async_remote_copy(
            src_ref=ref, dst_ref=ref, send_sem=ag_send.at[m, k], recv_sem=ag_recv.at[m, k],
            device_id=to, device_id_type=MESH,
        )

    def sb(m, k):
        b, rows = (
            (b_own, XR), (b_own, GR), (b_left, XR), (b_left, GR), (b_right, GR), (b_right, XR), (b_opp, XR), (b_opp, GR),
        )[k]
        ref = gath[m].at[:, b, rows]
        return pltpu.make_async_remote_copy(
            src_ref=ref, dst_ref=ref, send_sem=sib_send.at[m, k], recv_sem=sib_recv.at[m, k],
            device_id=sibling, device_id_type=MESH,
        )

    def scale(m, blocks):
        for b in blocks:
            s = scol_v[m, b]
            for f in range(NB):
                p_v[m, f, b] = (gath[m][f, b, SR:].astype(F32) * s).astype(BF)

    def ag_start(m):
        for k in (0, 2, 1, 3):
            go(ag, m, k)
        go(sb, m, 0)
        go(sb, m, 1)

    def ag_relay(m):
        got(ag, m, 0)
        go(ag, m, 4)
        go(sb, m, 2)
        got(ag, m, 2)
        go(ag, m, 5)
        go(sb, m, 4)
        got(ag, m, 1)
        go(sb, m, 3)
        got(ag, m, 3)
        go(sb, m, 5)

    def ag_finish(m):
        scale(m, (b_own, b_left, b_right))
        got(ag, m, 4)
        go(sb, m, 6)
        got(ag, m, 5)
        go(sb, m, 7)
        for k in range(8):
            got(sb, m, k)
        scale(m, (b_opp,) + tuple(oc * RING + i for i in range(RING)))

    def picked_in(m, h):
        blocks = [gath[m][grows_s[m, k, h], :, :SR].reshape(M * SR, 128) for k in range(2)]
        return jnp.concatenate(blocks, axis=1)

    def picked_out(m, h):
        return jnp.concatenate([p_v[m, dcols_s[m, k, h]].reshape(M * SR, 128) for k in range(2)], axis=1)

    def compute(m):
        for h in range(HB):
            both = [jnp.concatenate([w[m, h, 0], w[m, h, 1]], axis=0) for w in (gate_v, up_v)]
            ab = dot(picked_in(m, h), jnp.concatenate(both, axis=1))
            a, b = ab[:, :128], ab[:, 128:]
            q = dot(picked_out(m, h), dt_v[m, h])
            sig = jax.nn.sigmoid(a)
            act = a * sig
            hid = (act * b).astype(BF)
            prod = hid.astype(F32) * q
            gsum_v[...] = prod if h == 0 else gsum_v[...] + prod
            ub = (q * act).astype(BF)
            ga = (q * b * sig * (1.0 + a * (1.0 - sig))).astype(BF)
            h_v[m, h] = hid
            a_v[m, h] = ga
            u_v[m, h] = ub
            r = dot(jnp.concatenate([ga, ub], axis=1), wt_v[m, h])
            for k in range(2):
                terms_v[2 * h + k] = r[:, k * 128 : (k + 1) * 128].reshape(2, M // 2 * SR, 128)

        def gathered(f, core):
            acc = jnp.zeros((M // 2 * SR, 128), F32)
            for h in range(HB):
                acc += terms_v[table_s[(m * HB + h) * NB + f], core]
            return acc.reshape(RING, SR, 128)

        @pl.loop(0, NB)
        def _(f):
            part[m][f] = gathered(f, oc).astype(BF)

        go(core_copy, m)

        @pl.loop(0, NB)
        def _(f):
            own[m][f] = gathered(f, c)

    def score_part(m):
        s = scol_v[m].reshape(M * SR, 128)[:, :1]
        total = jnp.sum(gsum_v[...], axis=1, keepdims=True) / jnp.where(s > 0.0, s, 1.0)
        gsx_send[m : m + 1, :cap] = jnp.sum(jnp.where(slot_mask(m), total, 0.0), axis=0, keepdims=True)

    def block_grads(m):
        @pl.loop(0, HB)
        def _(h):
            both = dot(picked_in(m, h), jnp.concatenate([a_v[m, h], u_v[m, h]], axis=1), ((0,), (0,)))
            down = dot(h_v[m, h], picked_out(m, h), ((0,), (0,)))
            for k in range(2):
                gg_out[m, h, k] = both[k * 128 : (k + 1) * 128, :128]
                gu_out[m, h, k] = both[k * 128 : (k + 1) * 128, 128:]
                gd_out[m, h, k] = down[:, k * 128 : (k + 1) * 128]

    def core_copy(m):
        return pltpu.make_async_remote_copy(
            src_ref=part[m], dst_ref=sib[m], send_sem=sib_send.at[m, 8], recv_sem=sib_recv.at[m, 8],
            device_id=sibling, device_id_type=MESH,
        )

    HA, HBH = slice(0, NB // 2), slice(NB // 2, NB)

    def rs_copy(m, k):
        return pltpu.make_async_remote_copy(
            src_ref=hop_send.at[m, k], dst_ref=hop_recv.at[m, k], send_sem=rs_send.at[m, k],
            recv_sem=rs_recv.at[m, k], device_id=left if k % 2 else right, device_id_type=MESH,
        )

    def pair_sum(m, step, half):
        xx = (x + step) % RING
        return own[m][half, xx] + sib[m][half, xx].astype(F32)

    def rs_start(m):
        got(core_copy, m)
        for k, step, half in ((0, 2, HA), (1, 2, HBH), (2, 1, HBH), (3, 3, HA)):
            hop_send[m, k] = pair_sum(m, step, half).astype(BF)
            go(rs_copy, m, k)

    def rs_middle(m):
        for k, step, half in ((4, 1, HA), (5, 3, HBH)):
            got(rs_copy, m, k - 4)
            hop_send[m, k] = (pair_sum(m, step, half) + hop_recv[m, k - 4].astype(F32)).astype(BF)
            go(rs_copy, m, k)

    def rs_finish(m):
        for k in (2, 3, 4, 5):
            got(rs_copy, m, k)
        half = NB // 2
        fst_v[:half] = (pair_sum(m, 0, HA) + hop_recv[m, 4].astype(F32) + hop_recv[m, 3].astype(F32)).astype(BF)
        fst_v[half:] = (pair_sum(m, 0, HBH) + hop_recv[m, 2].astype(F32) + hop_recv[m, 5].astype(F32)).astype(BF)
        shape = (16 * G, 8 * SR)
        row, col = iota(shape, 0), iota(shape, 1)
        pick = as_bf(col == ((row >> 1) & 7) * SR + (row >> 4) * 2 + (row & 1))
        for i in range(O // 128):
            lanes = jnp.concatenate([fst_v[o * (O // 128) + i] for o in range(8)], axis=0)
            send2[m, :, :, i * 128 : (i + 1) * 128] = dot(pick, lanes).astype(BF).reshape(G, 16, 128)
        go_all(p2_copy, G, m)
        back[m][e] = send2[m, e]

    def token_part(m):
        got(p2_copy, m)
        shape = (8 * E2, 16 * G)
        row, col = iota(shape, 0), iota(shape, 1)
        o, j, g = row >> log2(E2), (row >> log2(G)) & 1, row & (G - 1)
        vals = dot(as_bf(col == g * 16 + o * 2 + j), back[m][...].reshape(16 * G, O)).astype(BF)
        for o in range(8):
            lanes = slice(o * O, (o + 1) * O)
            rows = dot(hotm_v[m], vals[o * E2 : (o + 1) * E2], ((0,), (0,)))
            if m == 0:
                gt_v[:, lanes] = rows
            else:
                gt_out[:, lanes] = (gt_v[:, lanes] + rows).astype(BF)

    def scores_start():
        gsx_recv[d] = gsx_send[...]
        go_all(gs_copy, M)

    def scores_finish():
        got(gs_copy)
        gs = gsx_recv[0]
        for i in range(1, M):
            gs = gs + gsx_recv[i]
        gs_out[...] = gs[:2, :cap]

    def gs_copy(i):
        return pltpu.make_async_remote_copy(
            src_ref=gsx_send, dst_ref=gsx_recv.at[d], send_sem=gs_send.at[i], recv_sem=gs_recv.at[i],
            device_id=(e, (d + i) % M), device_id_type=MESH,
        )

    run = functools.partial
    stages = (
        prepare, run(retile, 0), run(ag_start, 0), run(retile, 1), run(ag_relay, 0), run(ag_start, 1), run(ag_finish, 0),
        run(compute, 0), run(ag_relay, 1), run(rs_start, 0), run(score_part, 0), run(block_grads, 0), run(rs_middle, 0),
        run(ag_finish, 1), run(compute, 1), run(score_part, 1), scores_start, run(rs_finish, 0), run(rs_start, 1),
        run(block_grads, 1), run(rs_middle, 1), run(token_part, 0), run(rs_finish, 1), scores_finish, run(token_part, 1),
    )
    for stage in stages:
        stage()

    for wait in leaving:
        wait()


def write_out(*refs):
    n = len(refs) // 2
    copies = [pltpu.make_async_copy(src, dst, refs[-1].at[k]) for k, (src, dst) in enumerate(zip(refs[:n], refs[n:]))]
    for cp in copies:
        cp.start()
    for cp in copies:
        cp.wait()


def on_device(tokens, grad_out, scores, chosen, gate_vals, up_vals, down_vals, gate_rows, down_cols):
    G, M = lax.axis_size("expert"), lax.axis_size("dp")
    T, D = tokens.shape
    HB = gate_vals.shape[1]
    cap = chosen.shape[1]
    dims = (G, M, D, T, HB)
    E2, SR, O, Q, NB = 2 * G, 2 * G, D // 8, D // 4, D // 128
    rows = M * SR
    hbm, vmem = (pl.BlockSpec(memory_space=s) for s in (pl.ANY, pltpu.VMEM))
    dma = pltpu.SemaphoreType.DMA
    sds, V = jax.ShapeDtypeStruct, pltpu.VMEM
    shapes = [((T, D), BF)] + [(gate_vals.shape, F32)] * 3 + [((2, cap), F32)]
    gate_rows, down_cols = (jnp.swapaxes(a, 1, 2) for a in (gate_rows, down_cols))
    args = (chosen, scores, gate_rows, down_cols, tokens, grad_out, gate_vals, up_vals, down_vals)
    results = pl.pallas_call(
        functools.partial(exchange, dims),
        out_shape=tuple(V(*s) for s in shapes),
        in_specs=[hbm] * 9,
        out_specs=(vmem,) * 5,
        scratch_shapes=[
            V(chosen.shape, I32),
            V((2, cap), F32),
            pltpu.SMEM(gate_rows.shape, I32),
            pltpu.SMEM(gate_rows.shape, I32),
            pltpu.SMEM((2 * HB * NB,), I32),
            V((T, D), BF),
            V((T, D), BF),
            V(gate_vals.shape, BF),
            V(gate_vals.shape, BF),
            V(gate_vals.shape, BF),
            V((2, HB, 256, 256), BF),
            V((2, HB, 256, 128), BF),
            V((2 * E2, T), BF),
            V((2, E2, T), BF),
            V((8, 4 * G, Q), BF),
            V(chosen.shape, I32),
            V((2, M, SR, 128), F32),
            V((rows, 128), F32),
            V((2 * HB + 1, 2, rows // 2, 128), F32),
            V((2, HB, rows, 128), BF),
            V((2, HB, rows, 128), BF),
            V((2, HB, rows, 128), BF),
            V((2, NB, M, SR, 128), BF),
            V((8, 128), F32),
            V((M, 8, 128), F32),
            V((T, D), F32),
        ]
        + [V((G, 16, Q), BF)] * 4
        + [V((NB, M, 2 * SR, 128), BF)] * 2
        + [V((NB, RING, SR, 128), BF)] * 2
        + [V((NB, RING, SR, 128), F32)] * 2
        + [V((NB, RING, SR, 128), BF)] * 2
        + [V((2, 6, NB // 2, SR, 128), BF)] * 2
        + [V((NB, SR, 128), BF), V((2, G, 16, O), BF)]
        + [V((G, 16, O), BF)] * 2
        + [dma((9,))]
        + [dma((2, G))] * 2
        + [dma((2, 6))] * 2
        + [dma((2, 9))] * 2
        + [dma((2, 6))] * 2
        + [dma((2, G))] * 2
        + [dma((M,))] * 2,
        compiler_params=pltpu.CompilerParams(
            collective_id=0, has_side_effects=True, vmem_limit_bytes=44 * 1024 * 1024
        ),
        name="exchange",
    )(*(pltpu.with_memory_space_constraint(a, pltpu.HBM) for a in args))
    return pl.pallas_call(
        write_out,
        out_shape=tuple(sds(*s) for s in shapes),
        in_specs=[vmem] * 5,
        out_specs=(hbm,) * 5,
        scratch_shapes=[dma((5,))],
        compiler_params=pltpu.CompilerParams(vmem_limit_bytes=16 * 1024 * 1024),
        name="write_out",
    )(*(pltpu.with_memory_space_constraint(r, pltpu.VMEM) for r in results))


def solution(mesh):
    rows = P(("expert", "dp"), None)
    blocks = P("expert", "dp", None, None, None)
    links = P("expert", "dp", None)
    return jax.shard_map(
        on_device,
        mesh=mesh,
        in_specs=(rows, rows, P("expert", None), P(), blocks, blocks, blocks, links, links),
        out_specs=(rows, blocks, blocks, blocks, P("expert", None)),
        check_vma=False,
    )
```

```python
import functools

import jax
import jax.numpy as jnp
from jax import lax
from jax.experimental import pallas as pl
from jax.experimental.pallas import tpu as pltpu
from jax.sharding import PartitionSpec as P

MESH = pl.DeviceIdType.MESH
BF, F32, I32 = jnp.bfloat16, jnp.float32, jnp.int32
RING = 4


def iota(shape, dim):
    return lax.broadcasted_iota(I32, shape, dim)


def as_bf(mask):
    return jnp.where(mask, 1.0, 0.0).astype(BF)


def dot(a, b, dims=((1,), (0,))):
    return lax.dot_general(a, b, (dims, ((), ())), preferred_element_type=F32)


def same_int(a, b):
    return -(((a - b) * (a - b) - 1) >> 31)


def log2(n):
    return n.bit_length() - 1


def exchange(
    dims, chosen_hbm, scores_hbm, grows_hbm, dcols_hbm, tokens_hbm, grads_hbm, gate_hbm, up_hbm, down_hbm,
    gt_out, gg_out, gu_out, gd_out, gs_out,
    chosen_v, scores_v, grows_s, dcols_s, table_s, tok_v, grd_v, gate_v, up_v, down_v, wt_v, dt_v, hot_v, hotm_v, base_v,
    slot_v, scol_v, gsum_v, terms_v, h_v, a_v, u_v, p_v, gsx_send, gsx_recv, gt_v,
    send1_0, send1_1, recv1_0, recv1_1, gath_0, gath_1, part_0, part_1, own_0, own_1, sib_0, sib_1,
    hop_send, hop_recv, fst_v, send2, back_0, back_1,
    load_sem, p1_send, p1_recv, ag_send, ag_recv, sib_send, sib_recv, rs_send, rs_recv,
    p2_send, p2_recv, gs_send, gs_recv,
):
    G, M, D, T, HB = dims
    E2 = 2 * G
    SR = 2 * G
    Q, O = D // 4, D // 8
    NB = D // 128
    send1, recv1 = (send1_0, send1_1), (recv1_0, recv1_1)
    gath, part, own = (gath_0, gath_1), (part_0, part_1), (own_0, own_1)
    sib, back = (sib_0, sib_1), (back_0, back_1)

    e, d = lax.axis_index("expert"), lax.axis_index("dp")
    x, c = d // 2, d % 2
    oc = 1 - c
    right = (e, ((x + 1) % RING) * 2 + c)
    left = (e, ((x + 3) % RING) * 2 + c)
    sibling = (e, x * 2 + oc)
    b_own = c * RING + x
    b_right = c * RING + (x + 1) % RING
    b_left = c * RING + (x + 3) % RING
    b_opp = c * RING + (x + 2) % RING

    barrier = pltpu.get_barrier_semaphore()

    @pl.loop(1, G)
    def _(i):
        pl.semaphore_signal(barrier, inc=1, device_id=((e + i) % G, d), device_id_type=MESH)

    @pl.loop(1, M)
    def _(i):
        pl.semaphore_signal(barrier, inc=1, device_id=(e, (d + i) % M), device_id_type=MESH)

    loads = []
    for k, (src, dst) in enumerate((
        (chosen_hbm, chosen_v), (tokens_hbm, tok_v), (grads_hbm, grd_v), (scores_hbm, scores_v), (grows_hbm, grows_s),
        (dcols_hbm, dcols_s), (gate_hbm, gate_v), (up_hbm, up_v), (down_hbm, down_v),
    )):
        loads.append(pltpu.make_async_copy(src, dst, load_sem.at[k]))
    for cp in loads[:6]:
        cp.start()

    loads[0].wait()
    chosen = chosen_v[...]
    cap = chosen.shape[1]
    lo = (e * M + d) * T
    pos = iota(chosen.shape, 1)
    before = jnp.sum(jnp.where(chosen < lo, 1, 0), axis=1, keepdims=True)
    count = jnp.sum(jnp.where(chosen < lo + T, 1, 0), axis=1, keepdims=True) - before
    tok_id = iota((E2, T), 1)
    for j in range(2):
        loc = jnp.sum(jnp.where(pos == before + j, chosen, 0), axis=1, keepdims=True) - lo
        loc = jnp.where(count > j, loc, -1)
        hot_v[j * E2 : (j + 1) * E2, :] = as_bf(tok_id == loc)

    hot = hot_v[...]
    for arr, src in enumerate((tok_v, grd_v)):
        loads[1 + arr].wait()
        for q in range(4):
            base_v[arr * 4 + q] = dot(hot, src[:, q * Q : (q + 1) * Q]).astype(BF)

    arriving, leaving = {}, []

    def go(make, *key):
        make(*key).start()
        arriving[make, key] = lambda: make(*key).wait_recv()
        leaving.append(lambda: make(*key).wait_send())

    def go_all(make, n, *key):
        @pl.loop(1, n)
        def _(i):
            make(*key, i).start()

        def arrive():
            @pl.loop(1, n)
            def _(i):
                make(*key, i).wait_recv()

        def leave():
            @pl.loop(1, n)
            def _(i):
                make(*key, i).wait_send()

        arriving[make, key] = arrive
        leaving.append(leave)

    def got(make, *key):
        arriving.pop((make, key))()

    def p1_copy(m, i):
        g = (e + i) % G
        return pltpu.make_async_remote_copy(
            src_ref=send1[m].at[g], dst_ref=recv1[m].at[e], send_sem=p1_send.at[m, i], recv_sem=p1_recv.at[m, i],
            device_id=(g, d), device_id_type=MESH,
        )

    def p2_copy(m, i):
        g = (e + i) % G
        return pltpu.make_async_remote_copy(
            src_ref=send2.at[m, g], dst_ref=back[m].at[e], send_sem=p2_send.at[m, i], recv_sem=p2_recv.at[m, i],
            device_id=(g, d), device_id_type=MESH,
        )

    stacked = base_v[...].reshape(8 * 2 * E2, Q)
    shape = (G * 16, 8 * 2 * E2)
    row, col = iota(shape, 0), iota(shape, 1)
    want = ((row >> 1) & 7) * (2 * E2) + (row & 1) * E2 + (row >> 4) * 2
    for m in range(2):
        send1[m][...] = dot(as_bf(col == want + m), stacked).astype(BF).reshape(G, 16, Q)
        if m == 0:
            pl.semaphore_wait(barrier, G - 1 + M - 1)
        go_all(p1_copy, G, m)
        recv1[m][e] = send1[m][e]
    for cp in loads[6:]:
        cp.start()

    def prepare():
        owner = lax.shift_right_logical(chosen, log2(T))
        same = jnp.where((pltpu.roll(owner, 1, 1) == owner) & (pos > 0), 1, 0)
        member = owner & (M - 1)
        group = lax.shift_right_logical(owner, log2(M))
        slot_v[...] = ((member & 1) * RING + lax.shift_right_logical(member, 1)) * SR + group * 2 + same
        for cp in loads[3:6]:
            cp.wait()
        for m in range(2):
            s = jnp.sum(jnp.where(slot_mask(m), scores_v[m : m + 1, :], 0.0), axis=1, keepdims=True)
            scol_v[m] = jnp.broadcast_to(s, (M * SR, 128)).reshape(M, SR, 128)
            row, col = iota((E2, 2 * E2), 0), iota((E2, 2 * E2), 1)
            pick = as_bf(col == (row >> log2(G)) * E2 + (row & (G - 1)) * 2 + m)
            hotm_v[m] = dot(pick, hot_v[...]).astype(BF)

    def prepare_table():
        @pl.loop(0, 2 * HB)
        def _(i):
            m, h = i // HB, i % HB
            g0, g1 = grows_s[m, 0, h], grows_s[m, 1, h]
            for f in range(NB):
                n0 = same_int(g0, f)
                n1 = (1 - n0) * same_int(g1, f)
                table_s[i * NB + f] = 2 * HB - n0 * (2 * HB - 2 * h) - n1 * (2 * HB - 2 * h - 1)

    def prepare_weights():
        for cp in loads[6:]:
            cp.wait()

        @pl.loop(0, 2 * HB)
        def _(i):
            m, h = i // HB, i % HB
            for k in range(2):
                span = slice(k * 128, (k + 1) * 128)
                wt_v[m, h, :128, span] = gate_v[m, h, k].T
                wt_v[m, h, 128:, span] = up_v[m, h, k].T
                dt_v[m, h, span, :] = down_v[m, h, k].T

        terms_v[2 * HB] = jnp.zeros((2, M // 2 * SR, 128), F32)
        gsx_send[...] = jnp.zeros_like(gsx_send)

    def slot_mask(m):
        return iota((M * SR, cap), 0) == slot_v[pl.ds(2 * e + m, 1), :]

    def retile(m):
        got(p1_copy, m)
        shape = (16 * G, 16 * G)
        row, col = iota(shape, 0), iota(shape, 1)
        q = row >> log2(4 * G)
        arr = (row >> log2(2 * G)) & 1
        src = (row >> 1) & (G - 1)
        pick = as_bf(col == src * 16 + arr * 8 + q * 2 + (row & 1))
        out = dot(pick, recv1[m][...].reshape(16 * G, Q)).astype(BF)
        per_q = NB // 4
        for q in range(4):
            for i in range(per_q):
                gath[m][q * per_q + i, b_own] = out[q * 4 * G : (q + 1) * 4 * G, i * 128 : (i + 1) * 128]

    XR, GR = pl.ds(0, SR), pl.ds(SR, SR)

    def ag(m, k):
        b, rows, to = (
            (b_own, XR, right), (b_own, GR, right), (b_own, GR, left), (b_own, XR, left),
            (b_left, XR, right), (b_right, GR, left),
        )[k]
        ref = gath[m].at[:, b, rows]
        return pltpu.make_async_remote_copy(
            src_ref=ref, dst_ref=ref, send_sem=ag_send.at[m, k], recv_sem=ag_recv.at[m, k],
            device_id=to, device_id_type=MESH,
        )

    def sb(m, k):
        b, rows = (
            (b_own, XR), (b_own, GR), (b_left, XR), (b_left, GR), (b_right, GR), (b_right, XR), (b_opp, XR), (b_opp, GR),
        )[k]
        ref = gath[m].at[:, b, rows]
        return pltpu.make_async_remote_copy(
            src_ref=ref, dst_ref=ref, send_sem=sib_send.at[m, k], recv_sem=sib_recv.at[m, k],
            device_id=sibling, device_id_type=MESH,
        )

    def scale(m, blocks):
        for b in blocks:
            s = scol_v[m, b]
            for f in range(NB):
                p_v[m, f, b] = (gath[m][f, b, SR:].astype(F32) * s).astype(BF)

    def ag_start(m):
        for k in (0, 2, 1, 3):
            go(ag, m, k)
        go(sb, m, 0)
        go(sb, m, 1)

    def ag_relay(m):
        got(ag, m, 0)
        go(ag, m, 4)
        go(sb, m, 2)
        got(ag, m, 2)
        go(ag, m, 5)
        go(sb, m, 4)
        got(ag, m, 1)
        go(sb, m, 3)
        got(ag, m, 3)
        go(sb, m, 5)

    def ag_opposite(m):
        scale(m, (b_own, b_left, b_right))
        got(ag, m, 4)
        go(sb, m, 6)
        got(ag, m, 5)
        go(sb, m, 7)

    def ag_finish(m):
        for k in range(8):
            got(sb, m, k)
        scale(m, (b_opp,) + tuple(oc * RING + i for i in range(RING)))

    def picked_in(m, h):
        blocks = [gath[m][grows_s[m, k, h], :, :SR].reshape(M * SR, 128) for k in range(2)]
        return jnp.concatenate(blocks, axis=1)

    def picked_out(m, h):
        return jnp.concatenate([p_v[m, dcols_s[m, k, h]].reshape(M * SR, 128) for k in range(2)], axis=1)

    def chain(m):
        for h in range(HB):
            both = [jnp.concatenate([w[m, h, 0], w[m, h, 1]], axis=0) for w in (gate_v, up_v)]
            ab = dot(picked_in(m, h), jnp.concatenate(both, axis=1))
            a, b = ab[:, :128], ab[:, 128:]
            q = dot(picked_out(m, h), dt_v[m, h])
            sig = jax.nn.sigmoid(a)
            act = a * sig
            hid = (act * b).astype(BF)
            prod = hid.astype(F32) * q
            gsum_v[...] = prod if h == 0 else gsum_v[...] + prod
            ub = (q * act).astype(BF)
            ga = (q * b * sig * (1.0 + a * (1.0 - sig))).astype(BF)
            h_v[m, h] = hid
            a_v[m, h] = ga
            u_v[m, h] = ub
            r = dot(jnp.concatenate([ga, ub], axis=1), wt_v[m, h])
            for k in range(2):
                terms_v[2 * h + k] = r[:, k * 128 : (k + 1) * 128].reshape(2, M // 2 * SR, 128)

    def gathered(m, f, core):
        acc = terms_v[table_s[m * HB * NB + f], core]
        for h in range(1, HB):
            acc += terms_v[table_s[(m * HB + h) * NB + f], core]
        return acc.reshape(RING, SR, 128)

    def sum_away(m):
        @pl.loop(0, NB, unroll=2)
        def _(f):
            part[m][f] = gathered(m, f, oc).astype(BF)

        go(core_copy, m)

    def sum_own(m):
        @pl.loop(0, NB, unroll=2)
        def _(f):
            own[m][f] = gathered(m, f, c)

    def score_part(m):
        s = scol_v[m].reshape(M * SR, 128)[:, :1]
        total = jnp.sum(gsum_v[...], axis=1, keepdims=True) / jnp.where(s > 0.0, s, 1.0)
        gsx_send[m : m + 1, :cap] = jnp.sum(jnp.where(slot_mask(m), total, 0.0), axis=0, keepdims=True)

    def block_grads(m, lo, hi):
        @pl.loop(lo, hi)
        def _(h):
            both = dot(picked_in(m, h), jnp.concatenate([a_v[m, h], u_v[m, h]], axis=1), ((0,), (0,)))
            down = dot(h_v[m, h], picked_out(m, h), ((0,), (0,)))
            for k in range(2):
                gg_out[m, h, k] = both[k * 128 : (k + 1) * 128, :128]
                gu_out[m, h, k] = both[k * 128 : (k + 1) * 128, 128:]
                gd_out[m, h, k] = down[:, k * 128 : (k + 1) * 128]

    def core_copy(m):
        return pltpu.make_async_remote_copy(
            src_ref=part[m], dst_ref=sib[m], send_sem=sib_send.at[m, 8], recv_sem=sib_recv.at[m, 8],
            device_id=sibling, device_id_type=MESH,
        )

    HA, HBH = slice(0, NB // 2), slice(NB // 2, NB)

    def rs_copy(m, k):
        return pltpu.make_async_remote_copy(
            src_ref=hop_send.at[m, k], dst_ref=hop_recv.at[m, k], send_sem=rs_send.at[m, k],
            recv_sem=rs_recv.at[m, k], device_id=left if k % 2 else right, device_id_type=MESH,
        )

    def pair_sum(m, step, half):
        xx = (x + step) % RING
        return own[m][half, xx] + sib[m][half, xx].astype(F32)

    def rs_start(m):
        got(core_copy, m)
        for k, step, half in ((0, 2, HA), (1, 2, HBH), (2, 1, HBH), (3, 3, HA)):
            hop_send[m, k] = pair_sum(m, step, half).astype(BF)
            go(rs_copy, m, k)

    def rs_middle(m):
        for k, step, half in ((4, 1, HA), (5, 3, HBH)):
            got(rs_copy, m, k - 4)
            hop_send[m, k] = (pair_sum(m, step, half) + hop_recv[m, k - 4].astype(F32)).astype(BF)
            go(rs_copy, m, k)

    def rs_finish(m):
        for k in (2, 3, 4, 5):
            got(rs_copy, m, k)
        half = NB // 2
        fst_v[:half] = (pair_sum(m, 0, HA) + hop_recv[m, 4].astype(F32) + hop_recv[m, 3].astype(F32)).astype(BF)
        fst_v[half:] = (pair_sum(m, 0, HBH) + hop_recv[m, 2].astype(F32) + hop_recv[m, 5].astype(F32)).astype(BF)
        shape = (16 * G, 8 * SR)
        row, col = iota(shape, 0), iota(shape, 1)
        pick = as_bf(col == ((row >> 1) & 7) * SR + (row >> 4) * 2 + (row & 1))
        for i in range(O // 128):
            lanes = jnp.concatenate([fst_v[o * (O // 128) + i] for o in range(8)], axis=0)
            send2[m, :, :, i * 128 : (i + 1) * 128] = dot(pick, lanes).astype(BF).reshape(G, 16, 128)
        go_all(p2_copy, G, m)
        back[m][e] = send2[m, e]

    def token_part(m):
        got(p2_copy, m)
        shape = (8 * E2, 16 * G)
        row, col = iota(shape, 0), iota(shape, 1)
        o, j, g = row >> log2(E2), (row >> log2(G)) & 1, row & (G - 1)
        vals = dot(as_bf(col == g * 16 + o * 2 + j), back[m][...].reshape(16 * G, O)).astype(BF)
        for o in range(8):
            lanes = slice(o * O, (o + 1) * O)
            rows = dot(hotm_v[m], vals[o * E2 : (o + 1) * E2], ((0,), (0,)))
            if m == 0:
                gt_v[:, lanes] = rows
            else:
                gt_out[:, lanes] = (gt_v[:, lanes] + rows).astype(BF)

    def scores_start():
        gsx_recv[d] = gsx_send[...]
        go_all(gs_copy, M)

    def scores_finish():
        got(gs_copy)
        gs = gsx_recv[0]
        for i in range(1, M):
            gs = gs + gsx_recv[i]
        gs_out[...] = gs[:2, :cap]

    def gs_copy(i):
        return pltpu.make_async_remote_copy(
            src_ref=gsx_send, dst_ref=gsx_recv.at[d], send_sem=gs_send.at[i], recv_sem=gs_recv.at[i],
            device_id=(e, (d + i) % M), device_id_type=MESH,
        )

    run = functools.partial
    stages = (
        prepare, run(retile, 0), run(ag_start, 0), prepare_weights, run(retile, 1), run(ag_start, 1), prepare_table,
        run(ag_relay, 0), run(ag_relay, 1), run(ag_opposite, 0), run(ag_finish, 0),
        run(chain, 0), run(score_part, 0), run(ag_opposite, 1), run(sum_away, 0), run(sum_own, 0), run(ag_finish, 1),
        run(chain, 1), run(sum_away, 1), run(sum_own, 1),
        run(rs_start, 0), run(rs_start, 1), run(score_part, 1), scores_start, run(block_grads, 0, 0, HB // 2),
        run(rs_middle, 0), run(rs_middle, 1), run(block_grads, 0, HB // 2, HB),
        run(rs_finish, 0), run(rs_finish, 1), run(block_grads, 1, 0, HB), scores_finish,
        run(token_part, 0), run(token_part, 1),
    )
    for stage in stages:
        stage()

    for wait in leaving:
        wait()


def write_out(*refs):
    n = len(refs) // 2
    copies = [pltpu.make_async_copy(src, dst, refs[-1].at[k]) for k, (src, dst) in enumerate(zip(refs[:n], refs[n:]))]
    for cp in copies:
        cp.start()
    for cp in copies:
        cp.wait()


def on_device(tokens, grad_out, scores, chosen, gate_vals, up_vals, down_vals, gate_rows, down_cols):
    G, M = lax.axis_size("expert"), lax.axis_size("dp")
    T, D = tokens.shape
    HB = gate_vals.shape[1]
    cap = chosen.shape[1]
    dims = (G, M, D, T, HB)
    E2, SR, O, Q, NB = 2 * G, 2 * G, D // 8, D // 4, D // 128
    rows = M * SR
    hbm, vmem = (pl.BlockSpec(memory_space=s) for s in (pl.ANY, pltpu.VMEM))
    dma = pltpu.SemaphoreType.DMA
    sds, V = jax.ShapeDtypeStruct, pltpu.VMEM
    shapes = [((T, D), BF)] + [(gate_vals.shape, F32)] * 3 + [((2, cap), F32)]
    gate_rows, down_cols = (jnp.swapaxes(a, 1, 2) for a in (gate_rows, down_cols))
    args = (chosen, scores, gate_rows, down_cols, tokens, grad_out, gate_vals, up_vals, down_vals)
    results = pl.pallas_call(
        functools.partial(exchange, dims),
        out_shape=tuple(V(*s) for s in shapes),
        in_specs=[hbm] * 9,
        out_specs=(vmem,) * 5,
        scratch_shapes=[
            V(chosen.shape, I32),
            V((2, cap), F32),
            pltpu.SMEM(gate_rows.shape, I32),
            pltpu.SMEM(gate_rows.shape, I32),
            pltpu.SMEM((2 * HB * NB,), I32),
            V((T, D), BF),
            V((T, D), BF),
            V(gate_vals.shape, BF),
            V(gate_vals.shape, BF),
            V(gate_vals.shape, BF),
            V((2, HB, 256, 256), BF),
            V((2, HB, 256, 128), BF),
            V((2 * E2, T), BF),
            V((2, E2, T), BF),
            V((8, 4 * G, Q), BF),
            V(chosen.shape, I32),
            V((2, M, SR, 128), F32),
            V((rows, 128), F32),
            V((2 * HB + 1, 2, rows // 2, 128), F32),
            V((2, HB, rows, 128), BF),
            V((2, HB, rows, 128), BF),
            V((2, HB, rows, 128), BF),
            V((2, NB, M, SR, 128), BF),
            V((8, 128), F32),
            V((M, 8, 128), F32),
            V((T, D), F32),
        ]
        + [V((G, 16, Q), BF)] * 4
        + [V((NB, M, 2 * SR, 128), BF)] * 2
        + [V((NB, RING, SR, 128), BF)] * 2
        + [V((NB, RING, SR, 128), F32)] * 2
        + [V((NB, RING, SR, 128), BF)] * 2
        + [V((2, 6, NB // 2, SR, 128), BF)] * 2
        + [V((NB, SR, 128), BF), V((2, G, 16, O), BF)]
        + [V((G, 16, O), BF)] * 2
        + [dma((9,))]
        + [dma((2, G))] * 2
        + [dma((2, 6))] * 2
        + [dma((2, 9))] * 2
        + [dma((2, 6))] * 2
        + [dma((2, G))] * 2
        + [dma((M,))] * 2,
        compiler_params=pltpu.CompilerParams(
            collective_id=0, has_side_effects=True, vmem_limit_bytes=44 * 1024 * 1024
        ),
        name="exchange",
    )(*(pltpu.with_memory_space_constraint(a, pltpu.HBM) for a in args))
    return pl.pallas_call(
        write_out,
        out_shape=tuple(sds(*s) for s in shapes),
        in_specs=[vmem] * 5,
        out_specs=(hbm,) * 5,
        scratch_shapes=[dma((5,))],
        compiler_params=pltpu.CompilerParams(vmem_limit_bytes=16 * 1024 * 1024),
        name="write_out",
    )(*(pltpu.with_memory_space_constraint(r, pltpu.VMEM) for r in results))


def solution(mesh):
    rows = P(("expert", "dp"), None)
    blocks = P("expert", "dp", None, None, None)
    links = P("expert", "dp", None)
    return jax.shard_map(
        on_device,
        mesh=mesh,
        in_specs=(rows, rows, P("expert", None), P(), blocks, blocks, blocks, links, links),
        out_specs=(rows, blocks, blocks, blocks, P("expert", None)),
        check_vma=False,
    )
```

```python
import functools

import jax
import jax.numpy as jnp
from jax import lax
from jax.experimental import pallas as pl
from jax.experimental.pallas import tpu as pltpu
from jax.sharding import PartitionSpec as P

MESH = pl.DeviceIdType.MESH
BF, F32, I32 = jnp.bfloat16, jnp.float32, jnp.int32
RING = 4


def iota(shape, dim):
    return lax.broadcasted_iota(I32, shape, dim)


def as_bf(mask):
    return jnp.where(mask, 1.0, 0.0).astype(BF)


def dot(a, b, dims=((1,), (0,))):
    return lax.dot_general(a, b, (dims, ((), ())), preferred_element_type=F32)


def same_int(a, b):
    return -(((a - b) * (a - b) - 1) >> 31)


def log2(n):
    return n.bit_length() - 1


def exchange(
    dims, chosen_hbm, scores_hbm, grows_hbm, dcols_hbm, tokens_hbm, grads_hbm, gate_hbm, up_hbm, down_hbm,
    gt_out, gg_out, gu_out, gd_out, gs_out,
    chosen_v, scores_v, grows_s, dcols_s, table_s, tok_v, grd_v, gate_v, up_v, down_v, wt_v, dt_v, hot_v, hotm_v, base_v,
    slot_v, scol_v, gsum_v, terms_v, h_v, a_v, u_v, p_v, gsx_send, gsx_recv, gt_v,
    send1_0, send1_1, recv1_0, recv1_1, gath_0, gath_1, part_0, part_1, own_0, own_1, sib_0, sib_1,
    hop_send, hop_recv, fst_v, send2, back_0, back_1,
    load_sem, p1_send, p1_recv, ag_send, ag_recv, sib_send, sib_recv, rs_send, rs_recv,
    p2_send, p2_recv, gs_send, gs_recv,
):
    G, M, D, T, HB = dims
    E2 = 2 * G
    SR = 2 * G
    Q, O = D // 4, D // 8
    NB = D // 128
    send1, recv1 = (send1_0, send1_1), (recv1_0, recv1_1)
    gath, part, own = (gath_0, gath_1), (part_0, part_1), (own_0, own_1)
    sib, back = (sib_0, sib_1), (back_0, back_1)

    e, d = lax.axis_index("expert"), lax.axis_index("dp")
    x, c = d // 2, d % 2
    oc = 1 - c
    right = (e, ((x + 1) % RING) * 2 + c)
    left = (e, ((x + 3) % RING) * 2 + c)
    sibling = (e, x * 2 + oc)
    b_own = c * RING + x
    b_right = c * RING + (x + 1) % RING
    b_left = c * RING + (x + 3) % RING
    b_opp = c * RING + (x + 2) % RING

    barrier = pltpu.get_barrier_semaphore()

    @pl.loop(1, G)
    def _(i):
        pl.semaphore_signal(barrier, inc=1, device_id=((e + i) % G, d), device_id_type=MESH)

    @pl.loop(1, M)
    def _(i):
        pl.semaphore_signal(barrier, inc=1, device_id=(e, (d + i) % M), device_id_type=MESH)

    loads = []
    for k, (src, dst) in enumerate((
        (chosen_hbm, chosen_v), (tokens_hbm, tok_v), (grads_hbm, grd_v), (scores_hbm, scores_v), (grows_hbm, grows_s),
        (dcols_hbm, dcols_s), (gate_hbm, gate_v), (up_hbm, up_v), (down_hbm, down_v),
    )):
        loads.append(pltpu.make_async_copy(src, dst, load_sem.at[k]))
    for cp in loads[:6]:
        cp.start()

    loads[0].wait()
    chosen = chosen_v[...]
    cap = chosen.shape[1]
    lo = (e * M + d) * T
    pos = iota(chosen.shape, 1)
    before = jnp.sum(jnp.where(chosen < lo, 1, 0), axis=1, keepdims=True)
    count = jnp.sum(jnp.where(chosen < lo + T, 1, 0), axis=1, keepdims=True) - before
    tok_id = iota((E2, T), 1)
    for j in range(2):
        loc = jnp.sum(jnp.where(pos == before + j, chosen, 0), axis=1, keepdims=True) - lo
        loc = jnp.where(count > j, loc, -1)
        hot_v[j * E2 : (j + 1) * E2, :] = as_bf(tok_id == loc)

    hot = hot_v[...]
    for arr, src in enumerate((tok_v, grd_v)):
        loads[1 + arr].wait()
        for q in range(4):
            base_v[arr * 4 + q] = dot(hot, src[:, q * Q : (q + 1) * Q]).astype(BF)

    arriving, leaving = {}, []

    def go(make, *key):
        make(*key).start()
        arriving[make, key] = lambda: make(*key).wait_recv()
        leaving.append(lambda: make(*key).wait_send())

    def go_all(make, n, *key):
        @pl.loop(1, n)
        def _(i):
            make(*key, i).start()

        def arrive():
            @pl.loop(1, n)
            def _(i):
                make(*key, i).wait_recv()

        def leave():
            @pl.loop(1, n)
            def _(i):
                make(*key, i).wait_send()

        arriving[make, key] = arrive
        leaving.append(leave)

    def got(make, *key):
        arriving.pop((make, key))()

    def p1_copy(m, i):
        g = (e + i) % G
        return pltpu.make_async_remote_copy(
            src_ref=send1[m].at[g], dst_ref=recv1[m].at[e], send_sem=p1_send.at[m, i], recv_sem=p1_recv.at[m, i],
            device_id=(g, d), device_id_type=MESH,
        )

    def p2_copy(m, i):
        g = (e + i) % G
        return pltpu.make_async_remote_copy(
            src_ref=send2.at[m, g], dst_ref=back[m].at[e], send_sem=p2_send.at[m, i], recv_sem=p2_recv.at[m, i],
            device_id=(g, d), device_id_type=MESH,
        )

    stacked = base_v[...].reshape(8 * 2 * E2, Q)
    shape = (G * 16, 8 * 2 * E2)
    row, col = iota(shape, 0), iota(shape, 1)
    want = ((row >> 1) & 7) * (2 * E2) + (row & 1) * E2 + (row >> 4) * 2
    for m in range(2):
        send1[m][...] = dot(as_bf(col == want + m), stacked).astype(BF).reshape(G, 16, Q)
        recv1[m][e] = send1[m][e]
        if m == 0:
            pl.semaphore_wait(barrier, G - 1 + M - 1)
            go_all(p1_copy, G, 0)
    for cp in loads[6:]:
        cp.start()

    def prepare():
        owner = lax.shift_right_logical(chosen, log2(T))
        same = jnp.where((pltpu.roll(owner, 1, 1) == owner) & (pos > 0), 1, 0)
        member = owner & (M - 1)
        group = lax.shift_right_logical(owner, log2(M))
        slot_v[...] = ((member & 1) * RING + lax.shift_right_logical(member, 1)) * SR + group * 2 + same
        for cp in loads[3:6]:
            cp.wait()
        for m in range(2):
            s = jnp.sum(jnp.where(slot_mask(m), scores_v[m : m + 1, :], 0.0), axis=1, keepdims=True)
            scol_v[m] = jnp.broadcast_to(s, (M * SR, 128)).reshape(M, SR, 128)
            row, col = iota((E2, 2 * E2), 0), iota((E2, 2 * E2), 1)
            pick = as_bf(col == (row >> log2(G)) * E2 + (row & (G - 1)) * 2 + m)
            hotm_v[m] = dot(pick, hot_v[...]).astype(BF)

    def prepare_table():
        @pl.loop(0, 2 * HB)
        def _(i):
            m, h = i // HB, i % HB
            g0, g1 = grows_s[m, 0, h], grows_s[m, 1, h]
            for f in range(NB):
                n0 = same_int(g0, f)
                n1 = (1 - n0) * same_int(g1, f)
                table_s[i * NB + f] = 2 * HB - n0 * (2 * HB - 2 * h) - n1 * (2 * HB - 2 * h - 1)

    def prepare_weights():
        for cp in loads[6:]:
            cp.wait()

        @pl.loop(0, 2 * HB)
        def _(i):
            m, h = i // HB, i % HB
            for k in range(2):
                span = slice(k * 128, (k + 1) * 128)
                wt_v[m, h, :128, span] = gate_v[m, h, k].T
                wt_v[m, h, 128:, span] = up_v[m, h, k].T
                dt_v[m, h, span, :] = down_v[m, h, k].T

        terms_v[2 * HB] = jnp.zeros((2, M // 2 * SR, 128), F32)
        gsx_send[...] = jnp.zeros_like(gsx_send)

    def slot_mask(m):
        return iota((M * SR, cap), 0) == slot_v[pl.ds(2 * e + m, 1), :]

    def retile(m):
        got(p1_copy, m)
        shape = (16 * G, 16 * G)
        row, col = iota(shape, 0), iota(shape, 1)
        q = row >> log2(4 * G)
        arr = (row >> log2(2 * G)) & 1
        src = (row >> 1) & (G - 1)
        pick = as_bf(col == src * 16 + arr * 8 + q * 2 + (row & 1))
        out = dot(pick, recv1[m][...].reshape(16 * G, Q)).astype(BF)
        per_q = NB // 4
        for q in range(4):
            for i in range(per_q):
                gath[m][q * per_q + i, b_own] = out[q * 4 * G : (q + 1) * 4 * G, i * 128 : (i + 1) * 128]

    XR, GR = pl.ds(0, SR), pl.ds(SR, SR)

    def ag(m, k):
        b, rows, to = (
            (b_own, XR, right), (b_own, GR, right), (b_own, GR, left), (b_own, XR, left),
            (b_left, XR, right), (b_right, GR, left),
        )[k]
        ref = gath[m].at[:, b, rows]
        return pltpu.make_async_remote_copy(
            src_ref=ref, dst_ref=ref, send_sem=ag_send.at[m, k], recv_sem=ag_recv.at[m, k],
            device_id=to, device_id_type=MESH,
        )

    def sb(m, k):
        b, rows = (
            (b_own, XR), (b_own, GR), (b_left, XR), (b_left, GR), (b_right, GR), (b_right, XR), (b_opp, XR), (b_opp, GR),
        )[k]
        ref = gath[m].at[:, b, rows]
        return pltpu.make_async_remote_copy(
            src_ref=ref, dst_ref=ref, send_sem=sib_send.at[m, k], recv_sem=sib_recv.at[m, k],
            device_id=sibling, device_id_type=MESH,
        )

    def scale(m, blocks):
        for b in blocks:
            s = scol_v[m, b]
            for f in range(NB):
                p_v[m, f, b] = (gath[m][f, b, SR:].astype(F32) * s).astype(BF)

    def ag_start(m):
        for k in (0, 2, 1, 3):
            go(ag, m, k)
        go(sb, m, 0)
        go(sb, m, 1)

    def ag_relay(m):
        got(ag, m, 0)
        go(ag, m, 4)
        go(sb, m, 2)
        got(ag, m, 2)
        go(ag, m, 5)
        go(sb, m, 4)
        got(ag, m, 1)
        go(sb, m, 3)
        got(ag, m, 3)
        go(sb, m, 5)

    def ag_opposite(m):
        scale(m, (b_own, b_left, b_right))
        got(ag, m, 4)
        go(sb, m, 6)
        got(ag, m, 5)
        go(sb, m, 7)

    def ag_finish(m):
        for k in range(8):
            got(sb, m, k)
        scale(m, (b_opp,) + tuple(oc * RING + i for i in range(RING)))

    def picked_in(m, h):
        blocks = [gath[m][grows_s[m, k, h], :, :SR].reshape(M * SR, 128) for k in range(2)]
        return jnp.concatenate(blocks, axis=1)

    def picked_out(m, h):
        return jnp.concatenate([p_v[m, dcols_s[m, k, h]].reshape(M * SR, 128) for k in range(2)], axis=1)

    def chain(m):
        for h in range(HB):
            both = [jnp.concatenate([w[m, h, 0], w[m, h, 1]], axis=0) for w in (gate_v, up_v)]
            ab = dot(picked_in(m, h), jnp.concatenate(both, axis=1))
            a, b = ab[:, :128], ab[:, 128:]
            q = dot(picked_out(m, h), dt_v[m, h])
            sig = jax.nn.sigmoid(a)
            act = a * sig
            hid = (act * b).astype(BF)
            prod = hid.astype(F32) * q
            gsum_v[...] = prod if h == 0 else gsum_v[...] + prod
            ub = (q * act).astype(BF)
            ga = (q * b * sig * (1.0 + a * (1.0 - sig))).astype(BF)
            h_v[m, h] = hid
            a_v[m, h] = ga
            u_v[m, h] = ub
            r = dot(jnp.concatenate([ga, ub], axis=1), wt_v[m, h])
            for k in range(2):
                terms_v[2 * h + k] = r[:, k * 128 : (k + 1) * 128].reshape(2, M // 2 * SR, 128)

    def gathered(m, f, core):
        acc = terms_v[table_s[m * HB * NB + f], core]
        for h in range(1, HB):
            acc += terms_v[table_s[(m * HB + h) * NB + f], core]
        return acc.reshape(RING, SR, 128)

    def sum_away(m):
        @pl.loop(0, NB, unroll=2)
        def _(f):
            part[m][f] = gathered(m, f, oc).astype(BF)

        go(core_copy, m)

    def sum_own(m):
        @pl.loop(0, NB, unroll=2)
        def _(f):
            own[m][f] = gathered(m, f, c)

    def score_part(m):
        s = scol_v[m].reshape(M * SR, 128)[:, :1]
        total = jnp.sum(gsum_v[...], axis=1, keepdims=True) / jnp.where(s > 0.0, s, 1.0)
        gsx_send[m : m + 1, :cap] = jnp.sum(jnp.where(slot_mask(m), total, 0.0), axis=0, keepdims=True)

    def block_grads(m, lo, hi):
        @pl.loop(lo, hi)
        def _(h):
            both = dot(picked_in(m, h), jnp.concatenate([a_v[m, h], u_v[m, h]], axis=1), ((0,), (0,)))
            down = dot(h_v[m, h], picked_out(m, h), ((0,), (0,)))
            for k in range(2):
                gg_out[m, h, k] = both[k * 128 : (k + 1) * 128, :128]
                gu_out[m, h, k] = both[k * 128 : (k + 1) * 128, 128:]
                gd_out[m, h, k] = down[:, k * 128 : (k + 1) * 128]

    def core_copy(m):
        return pltpu.make_async_remote_copy(
            src_ref=part[m], dst_ref=sib[m], send_sem=sib_send.at[m, 8], recv_sem=sib_recv.at[m, 8],
            device_id=sibling, device_id_type=MESH,
        )

    HA, HBH = slice(0, NB // 2), slice(NB // 2, NB)

    def rs_copy(m, k):
        return pltpu.make_async_remote_copy(
            src_ref=hop_send.at[m, k], dst_ref=hop_recv.at[m, k], send_sem=rs_send.at[m, k],
            recv_sem=rs_recv.at[m, k], device_id=left if k % 2 else right, device_id_type=MESH,
        )

    def pair_sum(m, step, half):
        xx = (x + step) % RING
        return own[m][half, xx] + sib[m][half, xx].astype(F32)

    def rs_start(m):
        got(core_copy, m)
        for k, step, half in ((0, 2, HA), (1, 2, HBH), (2, 1, HBH), (3, 3, HA)):
            hop_send[m, k] = pair_sum(m, step, half).astype(BF)
            go(rs_copy, m, k)

    def rs_middle(m):
        for k, step, half in ((4, 1, HA), (5, 3, HBH)):
            got(rs_copy, m, k - 4)
            hop_send[m, k] = (pair_sum(m, step, half) + hop_recv[m, k - 4].astype(F32)).astype(BF)
            go(rs_copy, m, k)

    def rs_finish(m):
        for k in (2, 3, 4, 5):
            got(rs_copy, m, k)
        half = NB // 2
        fst_v[:half] = (pair_sum(m, 0, HA) + hop_recv[m, 4].astype(F32) + hop_recv[m, 3].astype(F32)).astype(BF)
        fst_v[half:] = (pair_sum(m, 0, HBH) + hop_recv[m, 2].astype(F32) + hop_recv[m, 5].astype(F32)).astype(BF)
        shape = (16 * G, 8 * SR)
        row, col = iota(shape, 0), iota(shape, 1)
        pick = as_bf(col == ((row >> 1) & 7) * SR + (row >> 4) * 2 + (row & 1))
        for i in range(O // 128):
            lanes = jnp.concatenate([fst_v[o * (O // 128) + i] for o in range(8)], axis=0)
            send2[m, :, :, i * 128 : (i + 1) * 128] = dot(pick, lanes).astype(BF).reshape(G, 16, 128)
        go_all(p2_copy, G, m)
        back[m][e] = send2[m, e]

    def token_part(m):
        got(p2_copy, m)
        shape = (8 * E2, 16 * G)
        row, col = iota(shape, 0), iota(shape, 1)
        o, j, g = row >> log2(E2), (row >> log2(G)) & 1, row & (G - 1)
        vals = dot(as_bf(col == g * 16 + o * 2 + j), back[m][...].reshape(16 * G, O)).astype(BF)
        for o in range(8):
            lanes = slice(o * O, (o + 1) * O)
            rows = dot(hotm_v[m], vals[o * E2 : (o + 1) * E2], ((0,), (0,)))
            if m == 0:
                gt_v[:, lanes] = rows
            else:
                gt_out[:, lanes] = (gt_v[:, lanes] + rows).astype(BF)

    def scores_start():
        gsx_recv[d] = gsx_send[...]
        go_all(gs_copy, M)

    def scores_finish():
        got(gs_copy)
        gs = gsx_recv[0]
        for i in range(1, M):
            gs = gs + gsx_recv[i]
        gs_out[...] = gs[:2, :cap]

    def gs_copy(i):
        return pltpu.make_async_remote_copy(
            src_ref=gsx_send, dst_ref=gsx_recv.at[d], send_sem=gs_send.at[i], recv_sem=gs_recv.at[i],
            device_id=(e, (d + i) % M), device_id_type=MESH,
        )

    run = functools.partial
    stages = (
        prepare, run(retile, 0), run(ag_start, 0), run(go_all, p1_copy, G, 1), prepare_table, prepare_weights, run(retile, 1), run(ag_start, 1),
        run(ag_relay, 0), run(ag_relay, 1), run(ag_opposite, 0), run(ag_finish, 0),
        run(chain, 0), run(score_part, 0), run(ag_opposite, 1), run(sum_away, 0), run(sum_own, 0), run(ag_finish, 1),
        run(rs_start, 0), run(chain, 1), run(sum_away, 1), run(rs_middle, 0), run(sum_own, 1),
        run(rs_start, 1), run(score_part, 1), scores_start, run(block_grads, 0, 0, HB // 2),
        run(rs_middle, 1), run(rs_finish, 0), run(block_grads, 0, HB // 2, HB),
        run(rs_finish, 1), run(block_grads, 1, 0, HB), scores_finish,
        run(token_part, 0), run(token_part, 1),
    )
    for stage in stages:
        stage()

    for wait in leaving:
        wait()


def write_out(*refs):
    n = len(refs) // 2
    copies = [pltpu.make_async_copy(src, dst, refs[-1].at[k]) for k, (src, dst) in enumerate(zip(refs[:n], refs[n:]))]
    for cp in copies:
        cp.start()
    for cp in copies:
        cp.wait()


def on_device(tokens, grad_out, scores, chosen, gate_vals, up_vals, down_vals, gate_rows, down_cols):
    G, M = lax.axis_size("expert"), lax.axis_size("dp")
    T, D = tokens.shape
    HB = gate_vals.shape[1]
    cap = chosen.shape[1]
    dims = (G, M, D, T, HB)
    E2, SR, O, Q, NB = 2 * G, 2 * G, D // 8, D // 4, D // 128
    rows = M * SR
    hbm, vmem = (pl.BlockSpec(memory_space=s) for s in (pl.ANY, pltpu.VMEM))
    dma = pltpu.SemaphoreType.DMA
    sds, V = jax.ShapeDtypeStruct, pltpu.VMEM
    shapes = [((T, D), BF)] + [(gate_vals.shape, F32)] * 3 + [((2, cap), F32)]
    gate_rows, down_cols = (jnp.swapaxes(a, 1, 2) for a in (gate_rows, down_cols))
    args = (chosen, scores, gate_rows, down_cols, tokens, grad_out, gate_vals, up_vals, down_vals)
    results = pl.pallas_call(
        functools.partial(exchange, dims),
        out_shape=tuple(V(*s) for s in shapes),
        in_specs=[hbm] * 9,
        out_specs=(vmem,) * 5,
        scratch_shapes=[
            V(chosen.shape, I32),
            V((2, cap), F32),
            pltpu.SMEM(gate_rows.shape, I32),
            pltpu.SMEM(gate_rows.shape, I32),
            pltpu.SMEM((2 * HB * NB,), I32),
            V((T, D), BF),
            V((T, D), BF),
            V(gate_vals.shape, BF),
            V(gate_vals.shape, BF),
            V(gate_vals.shape, BF),
            V((2, HB, 256, 256), BF),
            V((2, HB, 256, 128), BF),
            V((2 * E2, T), BF),
            V((2, E2, T), BF),
            V((8, 4 * G, Q), BF),
            V(chosen.shape, I32),
            V((2, M, SR, 128), F32),
            V((rows, 128), F32),
            V((2 * HB + 1, 2, rows // 2, 128), F32),
            V((2, HB, rows, 128), BF),
            V((2, HB, rows, 128), BF),
            V((2, HB, rows, 128), BF),
            V((2, NB, M, SR, 128), BF),
            V((8, 128), F32),
            V((M, 8, 128), F32),
            V((T, D), F32),
        ]
        + [V((G, 16, Q), BF)] * 4
        + [V((NB, M, 2 * SR, 128), BF)] * 2
        + [V((NB, RING, SR, 128), BF)] * 2
        + [V((NB, RING, SR, 128), F32)] * 2
        + [V((NB, RING, SR, 128), BF)] * 2
        + [V((2, 6, NB // 2, SR, 128), BF)] * 2
        + [V((NB, SR, 128), BF), V((2, G, 16, O), BF)]
        + [V((G, 16, O), BF)] * 2
        + [dma((9,))]
        + [dma((2, G))] * 2
        + [dma((2, 6))] * 2
        + [dma((2, 9))] * 2
        + [dma((2, 6))] * 2
        + [dma((2, G))] * 2
        + [dma((M,))] * 2,
        compiler_params=pltpu.CompilerParams(
            collective_id=0, has_side_effects=True, vmem_limit_bytes=44 * 1024 * 1024
        ),
        name="exchange",
    )(*(pltpu.with_memory_space_constraint(a, pltpu.HBM) for a in args))
    return pl.pallas_call(
        write_out,
        out_shape=tuple(sds(*s) for s in shapes),
        in_specs=[vmem] * 5,
        out_specs=(hbm,) * 5,
        scratch_shapes=[dma((5,))],
        compiler_params=pltpu.CompilerParams(vmem_limit_bytes=16 * 1024 * 1024),
        name="write_out",
    )(*(pltpu.with_memory_space_constraint(r, pltpu.VMEM) for r in results))


def solution(mesh):
    rows = P(("expert", "dp"), None)
    blocks = P("expert", "dp", None, None, None)
    links = P("expert", "dp", None)
    return jax.shard_map(
        on_device,
        mesh=mesh,
        in_specs=(rows, rows, P("expert", None), P(), blocks, blocks, blocks, links, links),
        out_specs=(rows, blocks, blocks, blocks, P("expert", None)),
        check_vma=False,
    )
```

```python
import functools

import jax
import jax.numpy as jnp
from jax import lax
from jax.experimental import pallas as pl
from jax.experimental.pallas import tpu as pltpu
from jax.sharding import PartitionSpec as P

MESH = pl.DeviceIdType.MESH
BF, F32, I32 = jnp.bfloat16, jnp.float32, jnp.int32
RING = 4


def iota(shape, dim):
    return lax.broadcasted_iota(I32, shape, dim)


def as_bf(mask):
    return jnp.where(mask, 1.0, 0.0).astype(BF)


def dot(a, b, dims=((1,), (0,))):
    return lax.dot_general(a, b, (dims, ((), ())), preferred_element_type=F32)


def same_int(a, b):
    return -(((a - b) * (a - b) - 1) >> 31)


def log2(n):
    return n.bit_length() - 1


def exchange(
    dims, chosen_hbm, scores_hbm, grows_hbm, dcols_hbm, tokens_hbm, grads_hbm, gate_hbm, up_hbm, down_hbm,
    gt_out, gg_out, gu_out, gd_out, gs_out,
    chosen_v, scores_v, grows_s, dcols_s, table_s, tok_v, grd_v, gate_v, up_v, down_v, wt_v, dt_v, hot_v, hotm_v, base_v,
    slot_v, scol_v, gsum_v, terms_v, h_v, a_v, u_v, p_v, gsx_send, gsx_recv, gt_v,
    send1_0, send1_1, recv1_0, recv1_1, gath_0, gath_1, part_0, part_1, own_0, own_1, sib_0, sib_1,
    hop_send, hop_recv, fst_v, send2, back_0, back_1,
    load_sem, p1_send, p1_recv, ag_send, ag_recv, sib_send, sib_recv, rs_send, rs_recv,
    p2_send, p2_recv, gs_send, gs_recv,
):
    G, M, D, T, HB = dims
    E2 = 2 * G
    SR = 2 * G
    Q, O = D // 4, D // 8
    NB = D // 128
    send1, recv1 = (send1_0, send1_1), (recv1_0, recv1_1)
    gath, part, own = (gath_0, gath_1), (part_0, part_1), (own_0, own_1)
    sib, back = (sib_0, sib_1), (back_0, back_1)

    e, d = lax.axis_index("expert"), lax.axis_index("dp")
    x, c = d // 2, d % 2
    oc = 1 - c
    right = (e, ((x + 1) % RING) * 2 + c)
    left = (e, ((x + 3) % RING) * 2 + c)
    sibling = (e, x * 2 + oc)
    b_own = c * RING + x
    b_right = c * RING + (x + 1) % RING
    b_left = c * RING + (x + 3) % RING
    b_opp = c * RING + (x + 2) % RING

    barrier = pltpu.get_barrier_semaphore()

    @pl.loop(1, G)
    def _(i):
        pl.semaphore_signal(barrier, inc=1, device_id=((e + i) % G, d), device_id_type=MESH)

    @pl.loop(1, M)
    def _(i):
        pl.semaphore_signal(barrier, inc=1, device_id=(e, (d + i) % M), device_id_type=MESH)

    loads = []
    for k, (src, dst) in enumerate((
        (chosen_hbm, chosen_v), (tokens_hbm, tok_v), (grads_hbm, grd_v), (scores_hbm, scores_v), (grows_hbm, grows_s),
        (dcols_hbm, dcols_s), (gate_hbm, gate_v), (up_hbm, up_v), (down_hbm, down_v),
    )):
        loads.append(pltpu.make_async_copy(src, dst, load_sem.at[k]))
    for cp in loads[:6]:
        cp.start()

    loads[0].wait()
    chosen = chosen_v[...]
    cap = chosen.shape[1]
    lo = (e * M + d) * T
    pos = iota(chosen.shape, 1)
    before = jnp.sum(jnp.where(chosen < lo, 1, 0), axis=1, keepdims=True)
    count = jnp.sum(jnp.where(chosen < lo + T, 1, 0), axis=1, keepdims=True) - before
    tok_id = iota((E2, T), 1)
    for j in range(2):
        loc = jnp.sum(jnp.where(pos == before + j, chosen, 0), axis=1, keepdims=True) - lo
        loc = jnp.where(count > j, loc, -1)
        hot_v[j * E2 : (j + 1) * E2, :] = as_bf(tok_id == loc)

    hot = hot_v[...]
    for arr, src in enumerate((tok_v, grd_v)):
        loads[1 + arr].wait()
        for q in range(4):
            base_v[arr * 4 + q] = dot(hot, src[:, q * Q : (q + 1) * Q]).astype(BF)

    arriving, leaving = {}, []

    def go(make, *key):
        make(*key).start()
        arriving[make, key] = lambda: make(*key).wait_recv()
        leaving.append(lambda: make(*key).wait_send())

    def go_all(make, n, *key):
        @pl.loop(1, n)
        def _(i):
            make(*key, i).start()

        def arrive():
            @pl.loop(1, n)
            def _(i):
                make(*key, i).wait_recv()

        def leave():
            @pl.loop(1, n)
            def _(i):
                make(*key, i).wait_send()

        arriving[make, key] = arrive
        leaving.append(leave)

    def got(make, *key):
        arriving.pop((make, key))()

    def p1_copy(m, i):
        g = (e + i) % G
        return pltpu.make_async_remote_copy(
            src_ref=send1[m].at[g], dst_ref=recv1[m].at[e], send_sem=p1_send.at[m, i], recv_sem=p1_recv.at[m, i],
            device_id=(g, d), device_id_type=MESH,
        )

    def p2_copy(m, i):
        g = (e + i) % G
        return pltpu.make_async_remote_copy(
            src_ref=send2.at[m, g], dst_ref=back[m].at[e], send_sem=p2_send.at[m, i], recv_sem=p2_recv.at[m, i],
            device_id=(g, d), device_id_type=MESH,
        )

    stacked = base_v[...].reshape(8 * 2 * E2, Q)
    shape = (G * 16, 8 * 2 * E2)
    row, col = iota(shape, 0), iota(shape, 1)
    want = ((row >> 1) & 7) * (2 * E2) + (row & 1) * E2 + (row >> 4) * 2
    for m in range(2):
        send1[m][...] = dot(as_bf(col == want + m), stacked).astype(BF).reshape(G, 16, Q)
        recv1[m][e] = send1[m][e]
        if m == 0:
            pl.semaphore_wait(barrier, G - 1 + M - 1)
            go_all(p1_copy, G, 0)
    for cp in loads[6:]:
        cp.start()

    def prepare():
        owner = lax.shift_right_logical(chosen, log2(T))
        same = jnp.where((pltpu.roll(owner, 1, 1) == owner) & (pos > 0), 1, 0)
        member = owner & (M - 1)
        group = lax.shift_right_logical(owner, log2(M))
        slot_v[...] = ((member & 1) * RING + lax.shift_right_logical(member, 1)) * SR + group * 2 + same
        for cp in loads[3:6]:
            cp.wait()
        for m in range(2):
            s = jnp.sum(jnp.where(slot_mask(m), scores_v[m : m + 1, :], 0.0), axis=1, keepdims=True)
            scol_v[m] = jnp.broadcast_to(s, (M * SR, 128)).reshape(M, SR, 128)
            row, col = iota((E2, 2 * E2), 0), iota((E2, 2 * E2), 1)
            pick = as_bf(col == (row >> log2(G)) * E2 + (row & (G - 1)) * 2 + m)
            hotm_v[m] = dot(pick, hot_v[...]).astype(BF)

    def prepare_table():
        @pl.loop(0, 2 * HB)
        def _(i):
            m, h = i // HB, i % HB
            g0, g1 = grows_s[m, 0, h], grows_s[m, 1, h]
            for f in range(NB):
                n0 = same_int(g0, f)
                n1 = (1 - n0) * same_int(g1, f)
                table_s[i * NB + f] = 2 * HB - n0 * (2 * HB - 2 * h) - n1 * (2 * HB - 2 * h - 1)

    def prepare_weights():
        for cp in loads[6:]:
            cp.wait()

        @pl.loop(0, 2 * HB)
        def _(i):
            m, h = i // HB, i % HB
            for k in range(2):
                span = slice(k * 128, (k + 1) * 128)
                wt_v[m, h, :128, span] = gate_v[m, h, k].T
                wt_v[m, h, 128:, span] = up_v[m, h, k].T
                dt_v[m, h, span, :] = down_v[m, h, k].T

        terms_v[2 * HB] = jnp.zeros((2, M // 2 * SR, 128), F32)
        gsx_send[...] = jnp.zeros_like(gsx_send)

    def slot_mask(m):
        return iota((M * SR, cap), 0) == slot_v[pl.ds(2 * e + m, 1), :]

    def retile(m):
        got(p1_copy, m)
        shape = (16 * G, 16 * G)
        row, col = iota(shape, 0), iota(shape, 1)
        q = row >> log2(4 * G)
        arr = (row >> log2(2 * G)) & 1
        src = (row >> 1) & (G - 1)
        pick = as_bf(col == src * 16 + arr * 8 + q * 2 + (row & 1))
        out = dot(pick, recv1[m][...].reshape(16 * G, Q)).astype(BF)
        per_q = NB // 4
        for q in range(4):
            for i in range(per_q):
                gath[m][q * per_q + i, b_own] = out[q * 4 * G : (q + 1) * 4 * G, i * 128 : (i + 1) * 128]

    XR, GR = pl.ds(0, SR), pl.ds(SR, SR)

    def ag(m, k):
        b, rows, to = (
            (b_own, XR, right), (b_own, GR, right), (b_own, GR, left), (b_own, XR, left),
            (b_left, XR, right), (b_right, GR, left),
        )[k]
        ref = gath[m].at[:, b, rows]
        return pltpu.make_async_remote_copy(
            src_ref=ref, dst_ref=ref, send_sem=ag_send.at[m, k], recv_sem=ag_recv.at[m, k],
            device_id=to, device_id_type=MESH,
        )

    def sb(m, k):
        b, rows = (
            (b_own, XR), (b_own, GR), (b_left, XR), (b_left, GR), (b_right, GR), (b_right, XR), (b_opp, XR), (b_opp, GR),
        )[k]
        ref = gath[m].at[:, b, rows]
        return pltpu.make_async_remote_copy(
            src_ref=ref, dst_ref=ref, send_sem=sib_send.at[m, k], recv_sem=sib_recv.at[m, k],
            device_id=sibling, device_id_type=MESH,
        )

    def scale(m, blocks):
        for b in blocks:
            s = scol_v[m, b]
            for f in range(NB):
                p_v[m, f, b] = (gath[m][f, b, SR:].astype(F32) * s).astype(BF)

    def ag_start(m):
        for k in (0, 2, 1, 3):
            go(ag, m, k)
        go(sb, m, 0)
        go(sb, m, 1)

    def ag_relay(m):
        got(ag, m, 0)
        go(ag, m, 4)
        go(sb, m, 2)
        got(ag, m, 2)
        go(ag, m, 5)
        go(sb, m, 4)
        got(ag, m, 1)
        go(sb, m, 3)
        got(ag, m, 3)
        go(sb, m, 5)

    def ag_opposite(m):
        scale(m, (b_own, b_left, b_right))
        got(ag, m, 4)
        go(sb, m, 6)
        got(ag, m, 5)
        go(sb, m, 7)

    def ag_finish(m):
        for k in range(8):
            got(sb, m, k)
        scale(m, (b_opp,) + tuple(oc * RING + i for i in range(RING)))

    def picked_in(m, h):
        blocks = [gath[m][grows_s[m, k, h], :, :SR].reshape(M * SR, 128) for k in range(2)]
        return jnp.concatenate(blocks, axis=1)

    def picked_out(m, h):
        return jnp.concatenate([p_v[m, dcols_s[m, k, h]].reshape(M * SR, 128) for k in range(2)], axis=1)

    def chain(m):
        for h in range(HB):
            both = [jnp.concatenate([w[m, h, 0], w[m, h, 1]], axis=0) for w in (gate_v, up_v)]
            ab = dot(picked_in(m, h), jnp.concatenate(both, axis=1))
            a, b = ab[:, :128], ab[:, 128:]
            q = dot(picked_out(m, h), dt_v[m, h])
            sig = jax.nn.sigmoid(a)
            act = a * sig
            hid = (act * b).astype(BF)
            prod = hid.astype(F32) * q
            gsum_v[m] = prod if h == 0 else gsum_v[m] + prod
            ub = (q * act).astype(BF)
            ga = (q * b * sig * (1.0 + a * (1.0 - sig))).astype(BF)
            h_v[m, h] = hid
            a_v[m, h] = ga
            u_v[m, h] = ub
            r = dot(jnp.concatenate([ga, ub], axis=1), wt_v[m, h])
            for k in range(2):
                terms_v[2 * h + k] = r[:, k * 128 : (k + 1) * 128].reshape(2, M // 2 * SR, 128)

    def gathered(m, f, core):
        acc = terms_v[table_s[m * HB * NB + f], core]
        for h in range(1, HB):
            acc += terms_v[table_s[(m * HB + h) * NB + f], core]
        return acc.reshape(RING, SR, 128)

    def sum_away(m):
        @pl.loop(0, NB, unroll=2)
        def _(f):
            part[m][f] = gathered(m, f, oc).astype(BF)

        go(core_copy, m)

    def sum_own(m):
        @pl.loop(0, NB, unroll=2)
        def _(f):
            own[m][f] = gathered(m, f, c)

    def score_part(m):
        s = scol_v[m].reshape(M * SR, 128)[:, :1]
        total = jnp.sum(gsum_v[m], axis=1, keepdims=True) / jnp.where(s > 0.0, s, 1.0)
        gsx_send[m : m + 1, :cap] = jnp.sum(jnp.where(slot_mask(m), total, 0.0), axis=0, keepdims=True)

    def block_grads(m, lo, hi):
        @pl.loop(lo, hi)
        def _(h):
            both = dot(picked_in(m, h), jnp.concatenate([a_v[m, h], u_v[m, h]], axis=1), ((0,), (0,)))
            down = dot(h_v[m, h], picked_out(m, h), ((0,), (0,)))
            for k in range(2):
                gg_out[m, h, k] = both[k * 128 : (k + 1) * 128, :128]
                gu_out[m, h, k] = both[k * 128 : (k + 1) * 128, 128:]
                gd_out[m, h, k] = down[:, k * 128 : (k + 1) * 128]

    def core_copy(m):
        return pltpu.make_async_remote_copy(
            src_ref=part[m], dst_ref=sib[m], send_sem=sib_send.at[m, 8], recv_sem=sib_recv.at[m, 8],
            device_id=sibling, device_id_type=MESH,
        )

    HA, HBH = slice(0, NB // 2), slice(NB // 2, NB)

    def rs_copy(m, k):
        return pltpu.make_async_remote_copy(
            src_ref=hop_send.at[m, k], dst_ref=hop_recv.at[m, k], send_sem=rs_send.at[m, k],
            recv_sem=rs_recv.at[m, k], device_id=left if k % 2 else right, device_id_type=MESH,
        )

    def pair_sum(m, step, half):
        xx = (x + step) % RING
        return own[m][half, xx] + sib[m][half, xx].astype(F32)

    def rs_start(m):
        got(core_copy, m)
        for k, step, half in ((0, 2, HA), (1, 2, HBH), (2, 1, HBH), (3, 3, HA)):
            hop_send[m, k] = pair_sum(m, step, half).astype(BF)
            go(rs_copy, m, k)

    def rs_middle(m):
        for k, step, half in ((4, 1, HA), (5, 3, HBH)):
            got(rs_copy, m, k - 4)
            hop_send[m, k] = (pair_sum(m, step, half) + hop_recv[m, k - 4].astype(F32)).astype(BF)
            go(rs_copy, m, k)

    def rs_finish(m):
        for k in (2, 3, 4, 5):
            got(rs_copy, m, k)
        half = NB // 2
        fst_v[:half] = (pair_sum(m, 0, HA) + hop_recv[m, 4].astype(F32) + hop_recv[m, 3].astype(F32)).astype(BF)
        fst_v[half:] = (pair_sum(m, 0, HBH) + hop_recv[m, 2].astype(F32) + hop_recv[m, 5].astype(F32)).astype(BF)
        shape = (16 * G, 8 * SR)
        row, col = iota(shape, 0), iota(shape, 1)
        pick = as_bf(col == ((row >> 1) & 7) * SR + (row >> 4) * 2 + (row & 1))
        for i in range(O // 128):
            lanes = jnp.concatenate([fst_v[o * (O // 128) + i] for o in range(8)], axis=0)
            send2[m, :, :, i * 128 : (i + 1) * 128] = dot(pick, lanes).astype(BF).reshape(G, 16, 128)
        go_all(p2_copy, G, m)
        back[m][e] = send2[m, e]

    def token_part(m):
        got(p2_copy, m)
        shape = (8 * E2, 16 * G)
        row, col = iota(shape, 0), iota(shape, 1)
        o, j, g = row >> log2(E2), (row >> log2(G)) & 1, row & (G - 1)
        vals = dot(as_bf(col == g * 16 + o * 2 + j), back[m][...].reshape(16 * G, O)).astype(BF)
        for o in range(8):
            lanes = slice(o * O, (o + 1) * O)
            rows = dot(hotm_v[m], vals[o * E2 : (o + 1) * E2], ((0,), (0,)))
            if m == 0:
                gt_v[:, lanes] = rows
            else:
                gt_out[:, lanes] = (gt_v[:, lanes] + rows).astype(BF)

    def scores_start():
        gsx_recv[d] = gsx_send[...]
        go_all(gs_copy, M)

    def scores_finish():
        got(gs_copy)
        gs = gsx_recv[0]
        for i in range(1, M):
            gs = gs + gsx_recv[i]
        gs_out[...] = gs[:2, :cap]

    def gs_copy(i):
        return pltpu.make_async_remote_copy(
            src_ref=gsx_send, dst_ref=gsx_recv.at[d], send_sem=gs_send.at[i], recv_sem=gs_recv.at[i],
            device_id=(e, (d + i) % M), device_id_type=MESH,
        )

    run = functools.partial
    stages = (
        prepare, run(retile, 0), run(ag_start, 0), run(go_all, p1_copy, G, 1), prepare_table, prepare_weights, run(retile, 1), run(ag_start, 1),
        run(ag_relay, 0), run(ag_relay, 1), run(ag_opposite, 0), run(ag_finish, 0),
        run(chain, 0), run(ag_opposite, 1), run(sum_away, 0), run(sum_own, 0), run(ag_finish, 1),
        run(rs_start, 0), run(chain, 1), run(sum_away, 1), run(rs_middle, 0), run(sum_own, 1),
        run(rs_start, 1), run(score_part, 0), run(score_part, 1), scores_start, run(block_grads, 0, 0, HB // 2),
        run(rs_middle, 1), run(rs_finish, 0), run(block_grads, 0, HB // 2, HB),
        run(rs_finish, 1), run(block_grads, 1, 0, HB), scores_finish,
        run(token_part, 0), run(token_part, 1),
    )
    for stage in stages:
        stage()

    for wait in leaving:
        wait()


def write_out(*refs):
    n = len(refs) // 2
    copies = [pltpu.make_async_copy(src, dst, refs[-1].at[k]) for k, (src, dst) in enumerate(zip(refs[:n], refs[n:]))]
    for cp in copies:
        cp.start()
    for cp in copies:
        cp.wait()


def on_device(tokens, grad_out, scores, chosen, gate_vals, up_vals, down_vals, gate_rows, down_cols):
    G, M = lax.axis_size("expert"), lax.axis_size("dp")
    T, D = tokens.shape
    HB = gate_vals.shape[1]
    cap = chosen.shape[1]
    dims = (G, M, D, T, HB)
    E2, SR, O, Q, NB = 2 * G, 2 * G, D // 8, D // 4, D // 128
    rows = M * SR
    hbm, vmem = (pl.BlockSpec(memory_space=s) for s in (pl.ANY, pltpu.VMEM))
    dma = pltpu.SemaphoreType.DMA
    sds, V = jax.ShapeDtypeStruct, pltpu.VMEM
    shapes = [((T, D), BF)] + [(gate_vals.shape, F32)] * 3 + [((2, cap), F32)]
    gate_rows, down_cols = (jnp.swapaxes(a, 1, 2) for a in (gate_rows, down_cols))
    args = (chosen, scores, gate_rows, down_cols, tokens, grad_out, gate_vals, up_vals, down_vals)
    results = pl.pallas_call(
        functools.partial(exchange, dims),
        out_shape=tuple(V(*s) for s in shapes),
        in_specs=[hbm] * 9,
        out_specs=(vmem,) * 5,
        scratch_shapes=[
            V(chosen.shape, I32),
            V((2, cap), F32),
            pltpu.SMEM(gate_rows.shape, I32),
            pltpu.SMEM(gate_rows.shape, I32),
            pltpu.SMEM((2 * HB * NB,), I32),
            V((T, D), BF),
            V((T, D), BF),
            V(gate_vals.shape, BF),
            V(gate_vals.shape, BF),
            V(gate_vals.shape, BF),
            V((2, HB, 256, 256), BF),
            V((2, HB, 256, 128), BF),
            V((2 * E2, T), BF),
            V((2, E2, T), BF),
            V((8, 4 * G, Q), BF),
            V(chosen.shape, I32),
            V((2, M, SR, 128), F32),
            V((2, rows, 128), F32),
            V((2 * HB + 1, 2, rows // 2, 128), F32),
            V((2, HB, rows, 128), BF),
            V((2, HB, rows, 128), BF),
            V((2, HB, rows, 128), BF),
            V((2, NB, M, SR, 128), BF),
            V((8, 128), F32),
            V((M, 8, 128), F32),
            V((T, D), F32),
        ]
        + [V((G, 16, Q), BF)] * 4
        + [V((NB, M, 2 * SR, 128), BF)] * 2
        + [V((NB, RING, SR, 128), BF)] * 2
        + [V((NB, RING, SR, 128), F32)] * 2
        + [V((NB, RING, SR, 128), BF)] * 2
        + [V((2, 6, NB // 2, SR, 128), BF)] * 2
        + [V((NB, SR, 128), BF), V((2, G, 16, O), BF)]
        + [V((G, 16, O), BF)] * 2
        + [dma((9,))]
        + [dma((2, G))] * 2
        + [dma((2, 6))] * 2
        + [dma((2, 9))] * 2
        + [dma((2, 6))] * 2
        + [dma((2, G))] * 2
        + [dma((M,))] * 2,
        compiler_params=pltpu.CompilerParams(
            collective_id=0, has_side_effects=True, vmem_limit_bytes=44 * 1024 * 1024
        ),
        name="exchange",
    )(*(pltpu.with_memory_space_constraint(a, pltpu.HBM) for a in args))
    return pl.pallas_call(
        write_out,
        out_shape=tuple(sds(*s) for s in shapes),
        in_specs=[vmem] * 5,
        out_specs=(hbm,) * 5,
        scratch_shapes=[dma((5,))],
        compiler_params=pltpu.CompilerParams(vmem_limit_bytes=16 * 1024 * 1024),
        name="write_out",
    )(*(pltpu.with_memory_space_constraint(r, pltpu.VMEM) for r in results))


def solution(mesh):
    rows = P(("expert", "dp"), None)
    blocks = P("expert", "dp", None, None, None)
    links = P("expert", "dp", None)
    return jax.shard_map(
        on_device,
        mesh=mesh,
        in_specs=(rows, rows, P("expert", None), P(), blocks, blocks, blocks, links, links),
        out_specs=(rows, blocks, blocks, blocks, P("expert", None)),
        check_vma=False,
    )
```
